256 devices in a mesh: dp: 16 (over z, core), tensor: 16 (over y, x).
Axes of the slice: x: 4, y: 4, z: 8, core: 2. Of those that a mesh axis runs over, the one named last changes fastest.
Arguments:
- gate_act: bfloat16 [6144, 14336], P('dp', 'tensor'), may hold values from -6 to 6
- up_act: bfloat16 [6144, 14336], P('dp', 'tensor'), may hold values from -6 to 6
- cotangent: bfloat16 [6144, 4096], P(('dp', 'tensor')), may hold values from -60 to 60
- frozen_weight: bfloat16 [14336, 4096], P('tensor'), may hold values from -1 to 1
- adapter_in: bfloat16 [64, 14336], P(None, 'tensor'), may hold values from -0.046875 to 0.046875
- adapter_out: bfloat16 [64, 4096], replicated, may hold values from -0.75 to 0.75
- magnitude: float32 [4096], replicated, may hold values from 1 to 8
Outputs:
- grad_gate: bfloat16 [6144, 14336], P('dp', 'tensor')
- grad_up: bfloat16 [6144, 14336], P('dp', 'tensor')
- grad_adapter_in: float32 [64, 14336], P(None, 'tensor')
- grad_adapter_out: float32 [64, 4096], replicated
- grad_magnitude: float32 [4096], replicated
The draws below stay inside these ranges and needn't reach their ends.
All inputs are finite; a program needn't handle non-finite values.
Results may differ from the reference program's by a relative error of at most 0.0075.
Values may be sent and summed in bfloat16 or wider, within the bound.
A program may use at most 128 MiB of HBM per device.

```python
import math
import jax
import jax.numpy as jnp
from jax import lax

D = 4096
FF = 14336
RANK = 64
TOKENS = 6144


def draw_frozen_weight(key, part):
    key = jax.random.fold_in(key, 11)
    key_entries, key_rows, key_columns = jax.random.split(key, 3)
    position = jnp.arange(FF, dtype=jnp.float32) / max(FF - 1, 1)
    row_scale = 10.0 ** (0.5 * position + 0.5 * jax.random.uniform(key_rows, (FF,), jnp.float32))
    column_scale = 10.0 ** jax.random.uniform(key_columns, (D,), jnp.float32)
    entries = jnp.clip(jax.random.normal(key_entries, (FF, D), jnp.float32), -5.0, 5.0)
    values = entries * row_scale[:, None] * column_scale[None, :] / (4.0 * math.sqrt(FF))
    return jnp.clip(values, -1.0, 1.0).astype(jnp.bfloat16)


def draw_cotangent(key, part):
    key = jax.random.fold_in(key, 23)
    key_entries, key_rows, key_columns = jax.random.split(key, 3)
    position = jnp.arange(TOKENS, dtype=jnp.float32) / max(TOKENS - 1, 1)
    row_scale = 10.0 ** (0.5 * position + 0.5 * jax.random.uniform(key_rows, (TOKENS,), jnp.float32))
    column_scale = 10.0 ** (jax.random.uniform(key_columns, (D,), jnp.float32) - 0.5)
    entries = jnp.clip(jax.random.normal(key_entries, (TOKENS, D), jnp.float32), -5.0, 5.0)
    values = entries * row_scale[:, None] * column_scale[None, :] / 3.0
    return jnp.clip(values, -60.0, 60.0).astype(jnp.bfloat16)


def shard_levels(key, dims, pieces, smallest, top_value):
    factor_of, own = 1.0, jax.random.fold_in(key, 6)
    for dim, blocks in pieces:
        heights = jnp.exp(jax.random.uniform(jax.random.fold_in(own, dim), (blocks,), jnp.float32, smallest / len(pieces), top_value / len(pieces)))
        factor_of = factor_of * jnp.repeat(heights, dims[dim] // blocks).reshape([-1 if axis == dim else 1 for axis in range(len(dims))])
    return factor_of


def noise(stream_key, dims, scale, most, cuts=(), kind=jnp.bfloat16):
    factor_of = shard_levels(stream_key, dims, cuts, -0.22, 0.18) if cuts else 1.0
    result = jax.random.normal(stream_key, dims, jnp.float32) * scale * factor_of
    return jnp.minimum(jnp.maximum(result, -most), most).astype(kind)


def setup_inputs(seed: int = 0) -> dict:
    splits = jax.random.split(jax.random.key(seed), 8)
    return {
        "gate_act": noise(splits[0], (TOKENS, FF), 1.0, 6.0, ((0, 16), (1, 16))),
        "up_act": noise(splits[1], (TOKENS, FF), 1.0, 6.0, ((0, 16), (1, 16))),
        "cotangent": draw_cotangent(jax.random.fold_in(splits[7], 71), 0),
        "frozen_weight": draw_frozen_weight(jax.random.fold_in(splits[7], 71), 0),
        "adapter_in": noise(splits[4], (RANK, FF), FF ** -0.5, 0.046875, ((1, 16),)),
        "adapter_out": noise(splits[5], (RANK, D), RANK ** -0.5, 0.75),
        "magnitude": jnp.clip(jnp.exp(jax.random.uniform(splits[6], (D,), jnp.float32, math.log(1.0), math.log(8.0))), 1.0, 8.0),
    }


epsilon = 1e-06

def reference(gate_act, up_act, cotangent, frozen_weight, adapter_in, adapter_out, magnitude):
    gate_value = gate_act.astype(jnp.float32)
    up_value = up_act.astype(jnp.float32)
    sigmoid_gate = jax.nn.sigmoid(gate_value)
    hidden = (gate_value * sigmoid_gate * up_value).astype(jnp.bfloat16)
    low_rank = jnp.dot(adapter_in.T, adapter_out, preferred_element_type=jnp.float32)
    adjusted = frozen_weight.astype(jnp.float32) + 2.0 * low_rank
    column_norm = jnp.sqrt(lax.optimization_barrier(jnp.sum(adjusted * adjusted, axis=0)) + epsilon)
    adjusted_low = adjusted.astype(jnp.bfloat16)
    column_scale = magnitude / column_norm
    scaled = (cotangent.astype(jnp.float32) * column_scale).astype(jnp.bfloat16)
    produced = jnp.dot(hidden, adjusted_low, preferred_element_type=jnp.float32)
    grad_magnitude = lax.optimization_barrier(jnp.sum(cotangent.astype(jnp.float32) * produced, axis=0)) / column_norm
    hidden_grad = jnp.dot(scaled, adjusted_low.T, preferred_element_type=jnp.float32)
    grad_up = (hidden_grad * gate_value * sigmoid_gate).astype(jnp.bfloat16)
    grad_gate = (hidden_grad * up_value * sigmoid_gate * (1.0 + gate_value * (1.0 - sigmoid_gate))).astype(jnp.bfloat16)
    rank_cot = jnp.dot(scaled, adapter_out.T, preferred_element_type=jnp.float32).astype(jnp.bfloat16)
    grad_adapter_in = 2.0 * jnp.dot(rank_cot.T, hidden, preferred_element_type=jnp.float32)
    projected = jnp.dot(hidden, adapter_in.T, preferred_element_type=jnp.float32)
    projected_high = projected.astype(jnp.bfloat16)
    projected_low = (projected - projected_high.astype(jnp.float32)).astype(jnp.bfloat16)
    out_high = jnp.dot(projected_high.T, scaled, preferred_element_type=jnp.float32)
    out_low = jnp.dot(projected_low.T, scaled, preferred_element_type=jnp.float32)
    grad_adapter_out = 2.0 * (out_high + out_low)
    return (grad_gate, grad_up, grad_adapter_in, grad_adapter_out, grad_magnitude)
```

```python
import jax
import jax.numpy as jnp
from jax import lax
from jax.experimental import pallas as pl
from jax.experimental.pallas import tpu as pltpu
from jax.sharding import PartitionSpec as P

epsilon = 1e-06
MESH = pl.DeviceIdType.MESH
f32 = jnp.float32
bf16 = jnp.bfloat16

LINE = 4
PEERS = LINE * LINE
GROUP = 16
DEPTH = GROUP // 2
ROWS = 24
TOK = ROWS * PEERS
F = 896
D = 4096
RANK = 64
HALF = D // 2
QUART = D // 4
COLS = D // PEERS
WBLK = 128
NWB = F // WBLK

(J, SQ_RS, SQ_AG, PR_RS, PR_AG, RC_AG, IN_RS, IN_AG, O_RS, O_PL, O_Z, O_CORE, M_RS, M_DP, M_AG) = range(15)
N_PHASES = 15


def dot(a, b, da, db):
    return lax.dot_general(a, b, (((da,), (db,)), ((), ())), preferred_element_type=f32)


def kernel(
    gate_h, up_h, cot_h, w_h, ain_h, aout_h, mag_h,
    ggate_h, gup_h, gin_h, gout_h, gmag_h,
    w_v, gate_v, up_v, hid_v, u_v, v_v, cot_v, ain_v, aout_v, mag_v, aint_v,
    cotb, scaled, prod, hg, sqacc, magacc, scale_v, norm_v,
    jsend, jrecv, sjv, sqp, sqr, sqf, prs, prr, pra, rcs, rca, lv,
    ipart, irecv, isum, iag, gin_v, opart, orecv, opl, ob, gout_v,
    magp, magr, magd, gmag_v, out_a, out_b,
    loc_sem, w_sem, out_sem, ph_send, ph_recv, g_send, g_recv,
):
    me_t = lax.axis_index("tensor")
    me_d = lax.axis_index("dp")
    x = lax.rem(me_t, LINE)
    y = lax.div(me_t, LINE)
    z = lax.div(me_d, 2)
    core = lax.rem(me_d, 2)

    loads = [
        pltpu.make_async_copy(cot_h, cot_v, loc_sem.at[0]),
        pltpu.make_async_copy(gate_h, gate_v, loc_sem.at[1]),
        pltpu.make_async_copy(up_h, up_v, loc_sem.at[2]),
        pltpu.make_async_copy(ain_h, ain_v.at[pl.ds(0, RANK)], loc_sem.at[3]),
        pltpu.make_async_copy(ain_h, ain_v.at[pl.ds(RANK, RANK)], loc_sem.at[4]),
        pltpu.make_async_copy(aout_h, aout_v.at[pl.ds(0, RANK)], loc_sem.at[5]),
        pltpu.make_async_copy(aout_h, aout_v.at[pl.ds(RANK, RANK)], loc_sem.at[6]),
        pltpu.make_async_copy(mag_h, mag_v, loc_sem.at[7]),
    ]
    for c in loads:
        c.start()

    def w_copy(i):
        rows = pl.ds(pl.multiple_of(i * WBLK, WBLK), WBLK)
        return pltpu.make_async_copy(w_h.at[rows], w_v.at[rows], w_sem.at[i])

    for i in range(NWB):
        w_copy(i).start()

    barrier = pltpu.get_barrier_semaphore()

    @pl.loop(1, PEERS)
    def _(d):
        pl.semaphore_signal(barrier, inc=1, device_id={"tensor": lax.rem(me_t + d, PEERS)}, device_id_type=MESH)

    @pl.loop(1, GROUP)
    def _(d):
        pl.semaphore_signal(barrier, inc=1, device_id={"dp": lax.rem(me_d + d, GROUP)}, device_id_type=MESH)

    loads[0].wait()
    for h in range(2):
        left = cot_v[:, HALF * h : HALF * h + QUART].astype(f32)
        right = cot_v[:, HALF * h + QUART : HALF * (h + 1)].astype(f32)
        cotb[h, me_t] = jnp.concatenate([left, right], axis=0).astype(bf16)
    for t in range(PEERS):
        left = cot_v[:, COLS * t : COLS * t + 128].astype(f32)
        right = cot_v[:, COLS * t + 128 : COLS * (t + 1)].astype(f32)
        jsend[t] = jnp.concatenate([left, right], axis=0).astype(bf16)
    jrecv[me_t] = jsend[me_t]

    pl.semaphore_wait(barrier, PEERS + GROUP - 2)

    def slot(h, along, across):
        if h == 0:
            return lax.rem(y + across + LINE, LINE) * LINE + lax.rem(x + along + LINE, LINE)
        return lax.rem(y + along + LINE, LINE) * LINE + lax.rem(x + across + LINE, LINE)

    def move(h, along, across, part, to, sem):
        if part is None:
            ref = cotb.at[h, slot(h, along, across)]
        else:
            ref = cotb.at[h, slot(h, along, across), :, pl.ds(part * (QUART // 2), QUART // 2)]
        return pltpu.make_async_remote_copy(
            src_ref=ref, dst_ref=ref, send_sem=g_send.at[20 * h + sem], recv_sem=g_recv.at[20 * h + sem],
            device_id={"tensor": to}, device_id_type=MESH,
        )

    sent = []

    def go(h, along, across, part, to, sem):
        c = move(h, along, across, part, to, sem)
        c.start()
        sent.append(c)

    def arrive(h, along, across, part, sem):
        move(h, along, across, part, slot(h, 0, 1), sem).wait_recv()

    offsets = (0, -1, 1, 2)

    def send_across(h, j):
        go(h, offsets[j], 0, None, slot(h, 0, 1), 4 + 4 * j)
        go(h, offsets[j], 0, None, slot(h, 0, -1), 5 + 4 * j)

    def forward_across(h, j):
        arrive(h, offsets[j], -1, None, 4 + 4 * j)
        go(h, offsets[j], -1, 0, slot(h, 0, 1), 6 + 4 * j)
        arrive(h, offsets[j], 1, None, 5 + 4 * j)
        go(h, offsets[j], 1, 1, slot(h, 0, -1), 7 + 4 * j)

    def last_across(h, j):
        arrive(h, offsets[j], 2, 0, 6 + 4 * j)
        arrive(h, offsets[j], 2, 1, 7 + 4 * j)

    for h in range(2):
        go(h, 0, 0, None, slot(h, 1, 0), 0)
        go(h, 0, 0, None, slot(h, -1, 0), 1)
    for h in range(2):
        send_across(h, 0)

    def exchange(phase, axis, src, dst, me, n):
        def one(p):
            return pltpu.make_async_remote_copy(
                src_ref=src(p), dst_ref=dst, send_sem=ph_send.at[phase], recv_sem=ph_recv.at[phase],
                device_id={axis: p}, device_id_type=MESH,
            )

        @pl.loop(1, n)
        def _(d):
            one(lax.rem(me + d, n)).start()

    def got(phase, ref):
        pltpu.make_async_copy(ref, ref, ph_recv.at[phase]).wait()

    def left_here(phase, ref):
        pltpu.make_async_copy(ref, ref, ph_send.at[phase]).wait()

    def to_plane(phase, src, dst):
        exchange(phase, "tensor", src, dst, me_t, PEERS)

    def to_group(phase, src, dst):
        exchange(phase, "dp", src, dst, me_d, GROUP)

    def my_cols(p):
        return pl.ds(pl.multiple_of(p * COLS, COLS), COLS)

    fifteen = pl.ds(0, 15)
    fifteen_cols = pl.ds(0, 15 * COLS)

    to_plane(J, lambda p: jsend.at[p], jrecv.at[me_t])

    loads[1].wait()
    loads[2].wait()

    @pl.loop(0, TOK // 16)
    def _(i):
        rows = pl.ds(pl.multiple_of(i * 16, 16), 16)
        g = gate_v[rows, :].astype(f32)
        u = up_v[rows, :].astype(f32)
        s = 1.0 / (1.0 + jnp.exp(-g))
        gs = g * s
        hid_v[rows, :] = (gs * u).astype(bf16)
        u_v[rows, :] = gs
        v_v[rows, :] = u * s * (1.0 + g * (1.0 - s))

    loads[3].wait()
    loads[4].wait()
    low_lanes = lax.broadcasted_iota(jnp.int32, (8, 128), 1) < RANK
    part = dot(hid_v[...], ain_v[...], 1, 1)
    for t in range(PEERS):
        r = ROWS * t
        prs[t, 0:8] = jnp.where(low_lanes, part[r : r + 8], part[r + 8 : r + 16])
        prs[t, 8:16] = part[r + 16 : r + 24]
    prr[me_t] = prs[me_t]
    to_plane(PR_RS, lambda p: prs.at[p], prr.at[me_t])

    aint_v[...] = (2.0 * jnp.transpose(ain_v[0:RANK, :].astype(f32), (1, 0))).astype(bf16)
    loads[5].wait()
    loads[6].wait()
    sqacc[...] = jnp.zeros_like(sqacc)

    def adjust(i):
        w_copy(i).wait()
        rows = pl.ds(pl.multiple_of(i * WBLK, WBLK), WBLK)
        lhs = aint_v[rows, :]
        for c in range(8):
            cols = slice(512 * c, 512 * (c + 1))
            a = w_v[rows, cols].astype(f32) + dot(lhs, aout_v[0:RANK, cols], 1, 0)
            w_v[rows, cols] = a.astype(bf16)
            sqacc[:, cols] += jnp.sum((a * a).reshape(WBLK // 8, 8, 512), axis=0)

    pl.loop(0, 4)(adjust)

    for h in range(2):
        arrive(h, -1, 0, None, 0)
        go(h, -1, 0, 0, slot(h, 1, 0), 2)
        arrive(h, 1, 0, None, 1)
        go(h, 1, 0, 1, slot(h, -1, 0), 3)
    for h in range(2):
        send_across(h, 1)
        send_across(h, 2)

    pl.loop(4, NWB)(adjust)

    sqp[...] = jnp.sum(sqacc[...], axis=0, keepdims=True)
    sqr[me_t] = sqp[:, my_cols(me_t)]
    to_plane(SQ_RS, lambda p: sqp.at[:, my_cols(p)], sqr.at[me_t])

    for h in range(2):
        forward_across(h, 0)

    got(PR_RS, prr.at[fifteen])
    total = prr[0]
    for t in range(1, PEERS):
        total = total + prr[t]
    pra[me_t] = total
    to_plane(PR_AG, lambda p: pra.at[me_t], pra.at[me_t])

    def produce(i):
        cols = pl.ds(pl.multiple_of(i * 256, 256), 256)
        prod[:, cols] = dot(hid_v[...], w_v[:, cols], 1, 0)

    pl.loop(0, 6)(produce)

    got(SQ_RS, sqr.at[fifteen])
    total = sqr[0]
    for t in range(1, PEERS):
        total = total + sqr[t]
    sqf[:, my_cols(me_t)] = total
    to_plane(SQ_AG, lambda p: sqf.at[:, my_cols(me_t)], sqf.at[:, my_cols(me_t)])

    for h in range(2):
        arrive(h, 2, 0, 0, 2)
        arrive(h, 2, 0, 1, 3)
        send_across(h, 3)

    pl.loop(6, 16)(produce)

    for h in range(2):
        forward_across(h, 1)
        forward_across(h, 2)

    loads[7].wait()
    got(SQ_AG, sqf.at[:, fifteen_cols])
    norm_v[...] = jnp.sqrt(sqf[...] + epsilon)
    scale_v[...] = mag_v[...] / norm_v[...]

    rank = jnp.zeros((32, 128), f32)
    for c in range(8):
        cols = slice(512 * c, 512 * (c + 1))
        s = cot_v[:, cols].astype(f32) * scale_v[:, cols]
        s = jnp.concatenate([s, jnp.zeros((8, 512), f32)], axis=0).astype(bf16)
        rank = rank + dot(s, aout_v[:, cols], 1, 1)
    rcs[...] = jnp.concatenate([jnp.where(low_lanes, rank[0:8], rank[8:16]), rank[16:24]], axis=0).astype(bf16)
    rca[me_t] = rcs[...]
    to_plane(RC_AG, lambda p: rcs, rca.at[me_t])

    got(J, jrecv.at[fifteen])
    got(PR_AG, pra.at[fifteen])
    scale_j = scale_v[:, my_cols(me_t)]
    for t in range(0, PEERS, 2):
        c0 = jrecv[t].astype(f32)
        c1 = jrecv[t + 1].astype(f32)
        left = jnp.concatenate([c0[0:24], c1[0:24]], axis=0) * scale_j[:, 0:128]
        right = jnp.concatenate([c0[24:48], c1[24:48]], axis=0) * scale_j[:, 128:256]
        sjv[ROWS * t : ROWS * (t + 2), 0:128] = left.astype(bf16)
        sjv[ROWS * t : ROWS * (t + 2), 128:256] = right.astype(bf16)

        def both(tile, last):
            turned = pltpu.roll(tile, RANK, 1)
            return [jnp.where(low_lanes, tile, turned), jnp.where(low_lanes, turned, tile), last]

        rows = jnp.concatenate(
            both(pra[t, 0:8], pra[t, 8:16]) + both(pra[t + 1, 0:8], pra[t + 1, 8:16]), axis=0
        )
        high = rows.astype(bf16).astype(f32)
        lanes = lax.broadcasted_iota(jnp.int32, rows.shape, 1) < RANK
        lv[ROWS * t : ROWS * (t + 2), :] = jnp.where(lanes, high, rows - high).astype(bf16)
    o = dot(lv[...], sjv[...], 0, 0)
    o = o[0:RANK] + o[RANK:]
    for p in range(GROUP):
        opart[p] = o[8 * (p // 2) : 8 * (p // 2) + 8, 128 * (p % 2) : 128 * (p % 2) + 128]
    orecv[me_d] = opart[me_d]
    to_group(O_RS, lambda p: opart.at[p], orecv.at[me_d])

    for h in range(2):
        forward_across(h, 3)

    got(RC_AG, rca.at[fifteen])
    for t in range(0, PEERS, 2):
        c0 = rca[t].astype(f32)
        c1 = rca[t + 1].astype(f32)
        rows = jnp.concatenate(
            [c0[0:8], pltpu.roll(c0[0:8], RANK, 1), c0[8:16], c1[0:8], pltpu.roll(c1[0:8], RANK, 1), c1[8:16]], axis=0
        )
        lv[ROWS * t : ROWS * (t + 2), :] = rows.astype(bf16)
    for g in range(4):
        w = 256 if g < 3 else 128
        o = dot(lv[...], hid_v[:, 256 * g : 256 * g + w], 0, 0)
        for b in range(4):
            ipart[4 * b + g, :, 0:w] = o[16 * b : 16 * b + 16]
            if w < 256:
                ipart[4 * b + g, :, w:256] = jnp.zeros((16, 256 - w), f32)
    irecv[me_d] = ipart[me_d]
    to_group(IN_RS, lambda p: ipart.at[p], irecv.at[me_d])

    magacc[...] = jnp.zeros_like(magacc)
    hg[...] = jnp.zeros_like(hg)
    CH = 256

    def rows_of(s):
        return pl.ds(pl.multiple_of(s * ROWS, ROWS), ROWS)

    def prepare(k):
        for h in range(2):
            for pair in range(2):
                if h == 0:
                    s0 = lax.rem(y + k + 3, LINE) * LINE + 2 * pair
                    s1 = s0 + 1
                else:
                    s0 = 2 * pair * LINE + lax.rem(x + k + 3, LINE)
                    s1 = s0 + LINE

                @pl.loop(0, QUART // CH)
                def _(c):
                    here = pl.ds(pl.multiple_of(c * CH, CH), CH)
                    c0 = cotb[h, s0, :, here].astype(f32)
                    c1 = cotb[h, s1, :, here].astype(f32)
                    for q in range(2):
                        a = c0[ROWS * q : ROWS * (q + 1)]
                        b = c1[ROWS * q : ROWS * (q + 1)]
                        at = pl.multiple_of(HALF * h + QUART * q + c * CH, CH)
                        cols = pl.ds(at, CH)
                        both = jnp.concatenate([a, b], axis=0) * scale_v[:, cols]
                        dst = pl.ds(pl.multiple_of(k * 96 + 48 * pair, 48), 48)
                        scaled[h, dst, pl.ds(pl.multiple_of(QUART * q + c * CH, CH), CH)] = both.astype(bf16)
                        m = a * prod[rows_of(s0), cols] + b * prod[rows_of(s1), cols]
                        magacc[:, cols] += jnp.sum(m.reshape(ROWS // 8, 8, CH), axis=0)

    def multiply(h, k0, n):
        for f in range(0, F, 256):
            w = min(256, F - f)
            r = dot(
                scaled[h, 96 * k0 : 96 * (k0 + n), :], w_v[f : f + w, HALF * h : HALF * (h + 1)], 1, 1
            )
            for k in range(k0, k0 + n):
                block = r[96 * (k - k0) : 96 * (k - k0 + 1)]
                if h == 0:
                    at = pl.multiple_of(lax.rem(y + k + 3, LINE) * 96, 96)
                    hg[pl.ds(at, 96), f : f + w] += block
                else:
                    for yy in range(LINE):
                        s = yy * LINE + lax.rem(x + k + 3, LINE)
                        hg[rows_of(s), f : f + w] += block[ROWS * yy : ROWS * (yy + 1)]

    for k in range(3):
        prepare(k)

    got(O_RS, orecv.at[fifteen])
    total = orecv[0]
    for t in range(1, GROUP):
        total = total + orecv[t]
    opl[me_t] = 2.0 * total
    to_plane(O_PL, lambda p: opl.at[me_t], opl.at[me_t])

    multiply(0, 0, 3)

    got(O_PL, opl.at[fifteen])
    ob[core, z] = opl[...].reshape(PEERS * 8, 128).astype(bf16)
    bundle = ob.at[core, z]

    @pl.loop(1, DEPTH)
    def _(d):
        pltpu.make_async_remote_copy(
            src_ref=bundle, dst_ref=bundle, send_sem=ph_send.at[O_Z], recv_sem=ph_recv.at[O_Z],
            device_id={"dp": lax.rem(z + d, DEPTH) * 2 + core}, device_id_type=MESH,
        ).start()

    got(IN_RS, irecv.at[fifteen])
    total = irecv[0]
    for t in range(1, GROUP):
        total = total + irecv[t]
    isum[...] = (2.0 * total).astype(bf16)
    iag[me_d] = isum[...]
    to_group(IN_AG, lambda p: isum, iag.at[me_d])

    multiply(1, 0, 3)

    for h in range(2):
        for j in range(4):
            last_across(h, j)
    prepare(3)
    magp[...] = jnp.sum(magacc[...], axis=0, keepdims=True)
    magr[me_t] = magp[:, my_cols(me_t)]
    to_plane(M_RS, lambda p: magp.at[:, my_cols(p)], magr.at[me_t])

    multiply(0, 3, 1)
    multiply(1, 3, 1)

    got(M_RS, magr.at[fifteen])
    total = magr[0]
    for t in range(1, PEERS):
        total = total + magr[t]
    magd[me_d] = total
    to_group(M_DP, lambda p: magd.at[me_d], magd.at[me_d])

    @pl.loop(0, TOK // 16)
    def _(i):
        rows = pl.ds(pl.multiple_of(i * 16, 16), 16)
        g = hg[rows, :]
        out_b[rows, :] = (g * u_v[rows, :]).astype(bf16)
        out_a[rows, :] = (g * v_v[rows, :]).astype(bf16)

    outs = [
        pltpu.make_async_copy(out_a, ggate_h, out_sem.at[0]),
        pltpu.make_async_copy(out_b, gup_h, out_sem.at[1]),
        pltpu.make_async_copy(gin_v, gin_h, out_sem.at[2]),
        pltpu.make_async_copy(gout_v, gout_h, out_sem.at[3]),
        pltpu.make_async_copy(gmag_v, gmag_h, out_sem.at[4]),
    ]
    outs[0].start()
    outs[1].start()

    got(O_Z, ob.at[0, pl.ds(0, DEPTH - 1)])
    other = pltpu.make_async_remote_copy(
        src_ref=ob.at[core], dst_ref=ob.at[core], send_sem=ph_send.at[O_CORE], recv_sem=ph_recv.at[O_CORE],
        device_id={"dp": z * 2 + 1 - core}, device_id_type=MESH,
    )
    other.start()

    got(M_DP, magd.at[fifteen])
    total = magd[0]
    for t in range(1, GROUP):
        total = total + magd[t]
    gmag_v[:, my_cols(me_t)] = total / norm_v[:, my_cols(me_t)]
    to_plane(M_AG, lambda p: gmag_v.at[:, my_cols(me_t)], gmag_v.at[:, my_cols(me_t)])

    got(IN_AG, iag.at[fifteen])
    for b in range(4):
        for g in range(4):
            w = 256 if g < 3 else 128
            gin_v[16 * b : 16 * b + 16, 256 * g : 256 * g + w] = iag[4 * b + g, :, 0:w].astype(f32)
    outs[2].start()

    other.wait_recv()
    for zz in range(DEPTH):
        for c in range(2):
            tile = ob[c, zz].astype(f32)
            for t in range(PEERS):
                at = COLS * t + 128 * c
                gout_v[8 * zz : 8 * zz + 8, at : at + 128] = tile[8 * t : 8 * t + 8]
    outs[3].start()

    got(M_AG, gmag_v.at[:, fifteen_cols])
    outs[4].start()

    for c in sent:
        c.wait_send()
    other.wait_send()
    left_here(J, jsend.at[fifteen])
    left_here(SQ_RS, sqp.at[:, fifteen_cols])
    left_here(SQ_AG, sqf.at[:, fifteen_cols])
    left_here(PR_RS, prs.at[fifteen])
    left_here(PR_AG, pra.at[fifteen])
    left_here(RC_AG, rca.at[fifteen])
    left_here(IN_RS, ipart.at[fifteen])
    left_here(IN_AG, iag.at[fifteen])
    left_here(O_RS, opart.at[fifteen])
    left_here(O_PL, opl.at[fifteen])
    left_here(O_Z, ob.at[0, pl.ds(0, DEPTH - 1)])
    left_here(M_RS, magp.at[:, fifteen_cols])
    left_here(M_DP, magd.at[fifteen])
    left_here(M_AG, gmag_v.at[:, fifteen_cols])
    for c in outs:
        c.wait()


def on_device(gate_act, up_act, cotangent, frozen_weight, adapter_in, adapter_out, magnitude):
    V = pltpu.VMEM
    scratch = [
        V((F, D), bf16), V((TOK, F), bf16), V((TOK, F), bf16), V((TOK, F), bf16),
        V((TOK, F), f32), V((TOK, F), f32), V((ROWS, D), bf16),
        V((2 * RANK, F), bf16), V((2 * RANK, D), bf16), V((1, D), f32), V((F, RANK), bf16),
        V((2, PEERS, 48, QUART), bf16), V((2, TOK, HALF), bf16), V((TOK, D), f32), V((TOK, F), f32),
        V((8, D), f32), V((8, D), f32), V((1, D), f32), V((1, D), f32),
        V((PEERS, 48, 128), bf16), V((PEERS, 48, 128), bf16), V((TOK, COLS), bf16),
        V((1, D), f32), V((PEERS, 1, COLS), f32), V((1, D), f32),
        V((PEERS, 16, 128), f32), V((PEERS, 16, 128), f32), V((PEERS, 16, 128), f32),
        V((16, 128), bf16), V((PEERS, 16, 128), bf16), V((TOK, 128), bf16),
        V((GROUP, 16, 256), f32), V((GROUP, 16, 256), f32), V((16, 256), bf16), V((GROUP, 16, 256), bf16),
        V((RANK, F), f32), V((GROUP, 8, 128), f32), V((GROUP, 8, 128), f32), V((PEERS, 8, 128), f32),
        V((2, DEPTH, 128, 128), bf16), V((RANK, D), f32),
        V((1, D), f32), V((PEERS, 1, COLS), f32), V((GROUP, 1, COLS), f32), V((1, D), f32),
        V((TOK, F), bf16), V((TOK, F), bf16),
        pltpu.SemaphoreType.DMA((8,)), pltpu.SemaphoreType.DMA((NWB,)), pltpu.SemaphoreType.DMA((5,)),
        pltpu.SemaphoreType.DMA((N_PHASES,)), pltpu.SemaphoreType.DMA((N_PHASES,)),
        pltpu.SemaphoreType.DMA((40,)), pltpu.SemaphoreType.DMA((40,)),
    ]
    hbm = pl.BlockSpec(memory_space=pl.ANY)
    outs = pl.pallas_call(
        kernel,
        out_shape=(
            jax.ShapeDtypeStruct((TOK, F), bf16),
            jax.ShapeDtypeStruct((TOK, F), bf16),
            jax.ShapeDtypeStruct((RANK, F), f32),
            jax.ShapeDtypeStruct((RANK, D), f32),
            jax.ShapeDtypeStruct((1, D), f32),
        ),
        in_specs=[hbm] * 7,
        out_specs=[hbm] * 5,
        scratch_shapes=scratch,
        compiler_params=pltpu.CompilerParams(
            collective_id=0, has_side_effects=True, vmem_limit_bytes=56 * 1024 * 1024
        ),
        cost_estimate=pl.CostEstimate(flops=7_000_000_000, bytes_accessed=14_000_000, transcendentals=400_000),
    )(gate_act, up_act, cotangent, frozen_weight, adapter_in, adapter_out, magnitude.reshape(1, D))
    return outs[0], outs[1], outs[2], outs[3], outs[4].reshape(D)


def solution(mesh):
    in_specs = (
        P("dp", "tensor"),
        P("dp", "tensor"),
        P(("dp", "tensor"), None),
        P("tensor", None),
        P(None, "tensor"),
        P(),
        P(),
    )
    out_specs = (P("dp", "tensor"), P("dp", "tensor"), P(None, "tensor"), P(), P())
    return jax.shard_map(
        on_device, mesh=mesh, in_specs=in_specs, out_specs=out_specs, check_vma=False
    )
```

```python
import jax
import jax.numpy as jnp
from jax import lax
from jax.experimental import pallas as pl
from jax.experimental.pallas import tpu as pltpu
from jax.sharding import PartitionSpec as P

epsilon = 1e-06
MESH = pl.DeviceIdType.MESH
f32 = jnp.float32
bf16 = jnp.bfloat16

LINE = 4
PEERS = LINE * LINE
GROUP = 16
DEPTH = GROUP // 2
ROWS = 24
TOK = ROWS * PEERS
F = 896
D = 4096
RANK = 64
HALF = D // 2
QUART = D // 4
COLS = D // PEERS
WBLK = 128
NWB = F // WBLK

(J, SQ_RS, SQ_AG, PR_RS, PR_AG, RC_AG, IN_RS, IN_AG, O_RS, O_PL, O_Z, O_CORE, M_RS, M_DP, M_AG) = range(15)
N_PHASES = 15


def dot(a, b, da, db):
    return lax.dot_general(a, b, (((da,), (db,)), ((), ())), preferred_element_type=f32)


def kernel(
    gate_h, up_h, cot_h, w_h, ain_h, aout_h, mag_h,
    ggate_h, gup_h, gin_h, gout_h, gmag_h,
    w_v, gate_v, up_v, hid_v, u_v, v_v, cot_v, ain_v, aout_v, mag_v, aint_v,
    cotb, scaled, prod, hg, sqacc, magacc, scale_v, norm_v,
    jsend, jrecv, sjv, sqp, sqr, sqf, prs, prr, pra, rcs, rca, lv,
    ipart, irecv, isum, iag, gin_v, opart, orecv, oz, ob, gout_v,
    magp, magr, magd, gmag_v, out_a, out_b,
    loc_sem, w_sem, out_sem, ph_send, ph_recv, g_send, g_recv,
):
    me_t = lax.axis_index("tensor")
    me_d = lax.axis_index("dp")
    x = lax.rem(me_t, LINE)
    y = lax.div(me_t, LINE)
    z = lax.div(me_d, 2)
    core = lax.rem(me_d, 2)

    loads = [
        pltpu.make_async_copy(cot_h, cot_v, loc_sem.at[0]),
        pltpu.make_async_copy(ain_h, ain_v.at[pl.ds(0, RANK)], loc_sem.at[1]),
        pltpu.make_async_copy(aout_h, aout_v.at[pl.ds(0, RANK)], loc_sem.at[2]),
        pltpu.make_async_copy(gate_h, gate_v, loc_sem.at[3]),
        pltpu.make_async_copy(up_h, up_v, loc_sem.at[4]),
        pltpu.make_async_copy(ain_h, ain_v.at[pl.ds(RANK, RANK)], loc_sem.at[5]),
        pltpu.make_async_copy(aout_h, aout_v.at[pl.ds(RANK, RANK)], loc_sem.at[6]),
        pltpu.make_async_copy(mag_h, mag_v, loc_sem.at[7]),
    ]

    def w_copy(i):
        rows = pl.ds(pl.multiple_of(i * WBLK, WBLK), WBLK)
        return pltpu.make_async_copy(w_h.at[rows], w_v.at[rows], w_sem.at[i])

    for c in loads[0:3]:
        c.start()
    for i in range(NWB):
        w_copy(i).start()
    for c in loads[3:]:
        c.start()

    barrier = pltpu.get_barrier_semaphore()

    @pl.loop(1, PEERS)
    def _(d):
        pl.semaphore_signal(barrier, inc=1, device_id={"tensor": lax.rem(me_t + d, PEERS)}, device_id_type=MESH)

    @pl.loop(1, GROUP)
    def _(d):
        pl.semaphore_signal(barrier, inc=1, device_id={"dp": lax.rem(me_d + d, GROUP)}, device_id_type=MESH)

    loads[0].wait()
    for h in range(2):
        left = cot_v[:, HALF * h : HALF * h + QUART].astype(f32)
        right = cot_v[:, HALF * h + QUART : HALF * (h + 1)].astype(f32)
        cotb[h, me_t] = jnp.concatenate([left, right], axis=0).astype(bf16)

    def slot(h, along, across):
        if h == 0:
            return lax.rem(y + across + LINE, LINE) * LINE + lax.rem(x + along + LINE, LINE)
        return lax.rem(y + along + LINE, LINE) * LINE + lax.rem(x + across + LINE, LINE)

    def move(h, along, across, part, to, sem):
        if part is None:
            ref = cotb.at[h, slot(h, along, across)]
        else:
            ref = cotb.at[h, slot(h, along, across), :, pl.ds(part * (QUART // 2), QUART // 2)]
        return pltpu.make_async_remote_copy(
            src_ref=ref, dst_ref=ref, send_sem=g_send.at[20 * h + sem], recv_sem=g_recv.at[20 * h + sem],
            device_id={"tensor": to}, device_id_type=MESH,
        )

    sent = []

    def go(h, along, across, part, to, sem):
        c = move(h, along, across, part, to, sem)
        c.start()
        sent.append(c)

    def arrive(h, along, across, part, sem):
        move(h, along, across, part, slot(h, 0, 1), sem).wait_recv()

    offsets = (0, -1, 1, 2)

    def send_across(h, j):
        go(h, offsets[j], 0, None, slot(h, 0, 1), 4 + 4 * j)
        go(h, offsets[j], 0, None, slot(h, 0, -1), 5 + 4 * j)

    def forward_across(h, j):
        arrive(h, offsets[j], -1, None, 4 + 4 * j)
        go(h, offsets[j], -1, 0, slot(h, 0, 1), 6 + 4 * j)
        arrive(h, offsets[j], 1, None, 5 + 4 * j)
        go(h, offsets[j], 1, 1, slot(h, 0, -1), 7 + 4 * j)

    def last_across(h, j):
        arrive(h, offsets[j], 2, 0, 6 + 4 * j)
        arrive(h, offsets[j], 2, 1, 7 + 4 * j)

    def exchange(phase, axis, src, dst, me, n):
        def one(p):
            return pltpu.make_async_remote_copy(
                src_ref=src(p), dst_ref=dst, send_sem=ph_send.at[phase], recv_sem=ph_recv.at[phase],
                device_id={axis: p}, device_id_type=MESH,
            )

        @pl.loop(1, n)
        def _(d):
            one(lax.rem(me + d, n)).start()

    def got(phase, ref):
        pltpu.make_async_copy(ref, ref, ph_recv.at[phase]).wait()

    def left_here(phase, ref):
        pltpu.make_async_copy(ref, ref, ph_send.at[phase]).wait()

    def to_plane(phase, src, dst):
        exchange(phase, "tensor", src, dst, me_t, PEERS)

    def to_group(phase, src, dst):
        exchange(phase, "dp", src, dst, me_d, GROUP)

    def my_cols(p):
        return pl.ds(pl.multiple_of(p * COLS, COLS), COLS)

    fifteen = pl.ds(0, 15)
    fifteen_cols = pl.ds(0, 15 * COLS)

    def sum_of(ref, n):
        total = ref[0]
        for t in range(1, n):
            total = total + ref[t]
        return total

    low_lanes = lax.broadcasted_iota(jnp.int32, (8, 128), 1) < RANK

    def gate_and_up():
        loads[3].wait()
        loads[4].wait()

        @pl.loop(0, TOK // 16)
        def _(i):
            rows = pl.ds(pl.multiple_of(i * 16, 16), 16)
            g = gate_v[rows, :].astype(f32)
            u = up_v[rows, :].astype(f32)
            s = 1.0 / (1.0 + jnp.exp(-g))
            gs = g * s
            hid_v[rows, :] = (gs * u).astype(bf16)
            u_v[rows, :] = gs
            v_v[rows, :] = u * s * (1.0 + g * (1.0 - s))

    def project():
        loads[5].wait()
        part = dot(hid_v[...], ain_v[...], 1, 1)
        for t in range(PEERS):
            r = ROWS * t
            prs[t, 0:8] = jnp.where(low_lanes, part[r : r + 8], part[r + 8 : r + 16])
            prs[t, 8:16] = part[r + 16 : r + 24]
        prr[me_t] = prs[me_t]
        to_plane(PR_RS, lambda p: prs.at[p], prr.at[me_t])

    def start_adjust():
        loads[1].wait()
        aint_v[...] = (2.0 * jnp.transpose(ain_v[0:RANK, :].astype(f32), (1, 0))).astype(bf16)
        sqacc[...] = jnp.zeros_like(sqacc)
        loads[2].wait()

    def adjust(i):
        w_copy(i).wait()
        rows = pl.ds(pl.multiple_of(i * WBLK, WBLK), WBLK)
        lhs = aint_v[rows, :]
        for c in range(8):
            cols = slice(512 * c, 512 * (c + 1))
            a = w_v[rows, cols].astype(f32) + dot(lhs, aout_v[0:RANK, cols], 1, 0)
            w_v[rows, cols] = a.astype(bf16)
            sqacc[:, cols] += jnp.sum((a * a).reshape(WBLK // 8, 8, 512), axis=0)

    def send_squares():
        sqp[...] = jnp.sum(sqacc[...], axis=0, keepdims=True)
        sqr[me_t] = sqp[:, my_cols(me_t)]
        to_plane(SQ_RS, lambda p: sqp.at[:, my_cols(p)], sqr.at[me_t])

    def sum_squares():
        got(SQ_RS, sqr.at[fifteen])
        sqf[:, my_cols(me_t)] = sum_of(sqr, PEERS)
        to_plane(SQ_AG, lambda p: sqf.at[:, my_cols(me_t)], sqf.at[:, my_cols(me_t)])

    def send_columns():
        for t in range(PEERS):
            left = cot_v[:, COLS * t : COLS * t + 128].astype(f32)
            right = cot_v[:, COLS * t + 128 : COLS * (t + 1)].astype(f32)
            jsend[t] = jnp.concatenate([left, right], axis=0).astype(bf16)
        jrecv[me_t] = jsend[me_t]
        to_plane(J, lambda p: jsend.at[p], jrecv.at[me_t])

    def first_along():
        for h in range(2):
            arrive(h, -1, 0, None, 0)
            go(h, -1, 0, 0, slot(h, 1, 0), 2)
            arrive(h, 1, 0, None, 1)
            go(h, 1, 0, 1, slot(h, -1, 0), 3)
        for h in range(2):
            send_across(h, 1)
            send_across(h, 2)

    def last_along():
        for h in range(2):
            arrive(h, 2, 0, 0, 2)
            arrive(h, 2, 0, 1, 3)
            send_across(h, 3)

    def sum_projected():
        got(PR_RS, prr.at[fifteen])
        pra[me_t] = sum_of(prr, PEERS)
        to_plane(PR_AG, lambda p: pra.at[me_t], pra.at[me_t])

    def produce(i):
        cols = pl.ds(pl.multiple_of(i * 256, 256), 256)
        prod[:, cols] = dot(hid_v[...], w_v[:, cols], 1, 0)

    def out_grad():
        got(J, jrecv.at[fifteen])
        got(PR_AG, pra.at[fifteen])
        for t in range(0, PEERS, 2):
            c0 = jrecv[t].astype(f32)
            c1 = jrecv[t + 1].astype(f32)
            sjv[ROWS * t : ROWS * (t + 2), 0:128] = jnp.concatenate([c0[0:24], c1[0:24]], axis=0).astype(bf16)
            sjv[ROWS * t : ROWS * (t + 2), 128:256] = jnp.concatenate([c0[24:48], c1[24:48]], axis=0).astype(bf16)

            def both(tile, last):
                turned = pltpu.roll(tile, RANK, 1)
                return [jnp.where(low_lanes, tile, turned), jnp.where(low_lanes, turned, tile), last]

            rows = jnp.concatenate(
                both(pra[t, 0:8], pra[t, 8:16]) + both(pra[t + 1, 0:8], pra[t + 1, 8:16]), axis=0
            )
            high = rows.astype(bf16).astype(f32)
            lanes = lax.broadcasted_iota(jnp.int32, rows.shape, 1) < RANK
            lv[ROWS * t : ROWS * (t + 2), :] = jnp.where(lanes, high, rows - high).astype(bf16)
        o = dot(lv[...], sjv[...], 0, 0)
        o = o[0:RANK] + o[RANK:]
        for p in range(GROUP):
            opart[p] = o[8 * (p // 2) : 8 * (p // 2) + 8, 128 * (p % 2) : 128 * (p % 2) + 128]
        orecv[me_d] = opart[me_d]
        to_group(O_RS, lambda p: opart.at[p], orecv.at[me_d])

    def sum_out_grad():
        got(O_RS, orecv.at[fifteen])
        mine = pl.ds(pl.multiple_of(me_t * COLS + core * 128, 128), 128)
        oz[z] = 2.0 * sum_of(orecv, GROUP) * scale_v[:, mine]

        @pl.loop(1, DEPTH)
        def _(d):
            pltpu.make_async_remote_copy(
                src_ref=oz.at[z], dst_ref=oz.at[z], send_sem=ph_send.at[O_Z], recv_sem=ph_recv.at[O_Z],
                device_id={"dp": lax.rem(z + d, DEPTH) * 2 + core}, device_id_type=MESH,
            ).start()

    def spread_out_grad():
        got(O_Z, oz.at[pl.ds(0, DEPTH - 1)])
        ob[core, me_t] = oz[...].reshape(RANK, 128).astype(bf16)
        to_plane(O_PL, lambda p: ob.at[core, me_t], ob.at[core, me_t])

    other = pltpu.make_async_remote_copy(
        src_ref=ob.at[core], dst_ref=ob.at[core], send_sem=ph_send.at[O_CORE], recv_sem=ph_recv.at[O_CORE],
        device_id={"dp": z * 2 + 1 - core}, device_id_type=MESH,
    )

    def swap_out_grad():
        got(O_PL, ob.at[0, fifteen])
        other.start()

    def column_scale():
        loads[7].wait()
        got(SQ_AG, sqf.at[:, fifteen_cols])
        norm_v[...] = jnp.sqrt(sqf[...] + epsilon)
        scale_v[...] = mag_v[...] / norm_v[...]

    def send_rank():
        loads[6].wait()
        rank = jnp.zeros((32, 128), f32)
        for c in range(8):
            cols = slice(512 * c, 512 * (c + 1))
            s = cot_v[:, cols].astype(f32) * scale_v[:, cols]
            s = jnp.concatenate([s, jnp.zeros((8, 512), f32)], axis=0).astype(bf16)
            rank = rank + dot(s, aout_v[:, cols], 1, 1)
        rcs[...] = jnp.concatenate([jnp.where(low_lanes, rank[0:8], rank[8:16]), rank[16:24]], axis=0).astype(bf16)
        rca[me_t] = rcs[...]
        to_plane(RC_AG, lambda p: rcs, rca.at[me_t])

    def in_grad():
        got(RC_AG, rca.at[fifteen])
        for t in range(0, PEERS, 2):
            c0 = rca[t].astype(f32)
            c1 = rca[t + 1].astype(f32)
            rows = jnp.concatenate(
                [c0[0:8], pltpu.roll(c0[0:8], RANK, 1), c0[8:16], c1[0:8], pltpu.roll(c1[0:8], RANK, 1), c1[8:16]], axis=0
            )
            lv[ROWS * t : ROWS * (t + 2), :] = rows.astype(bf16)
        for g in range(4):
            w = 256 if g < 3 else 128
            o = dot(lv[...], hid_v[:, 256 * g : 256 * g + w], 0, 0).astype(bf16)
            for b in range(4):
                ipart[4 * b + g, :, 0:w] = o[16 * b : 16 * b + 16]
                if w < 256:
                    ipart[4 * b + g, :, w:256] = jnp.zeros((16, 256 - w), bf16)
        irecv[me_d] = ipart[me_d]
        to_group(IN_RS, lambda p: ipart.at[p], irecv.at[me_d])

    def sum_in_grad():
        got(IN_RS, irecv.at[fifteen])
        total = irecv[0].astype(f32)
        for t in range(1, GROUP):
            total = total + irecv[t].astype(f32)
        isum[...] = (2.0 * total).astype(bf16)
        iag[me_d] = isum[...]
        to_group(IN_AG, lambda p: isum, iag.at[me_d])

    CH = 256

    def rows_of(s):
        return pl.ds(pl.multiple_of(s * ROWS, ROWS), ROWS)

    def prepare(k):
        for h in range(2):
            for pair in range(2):
                if h == 0:
                    s0 = lax.rem(y + k + 3, LINE) * LINE + 2 * pair
                    s1 = s0 + 1
                else:
                    s0 = 2 * pair * LINE + lax.rem(x + k + 3, LINE)
                    s1 = s0 + LINE

                @pl.loop(0, QUART // CH)
                def _(c):
                    here = pl.ds(pl.multiple_of(c * CH, CH), CH)
                    c0 = cotb[h, s0, :, here].astype(f32)
                    c1 = cotb[h, s1, :, here].astype(f32)
                    for q in range(2):
                        a = c0[ROWS * q : ROWS * (q + 1)]
                        b = c1[ROWS * q : ROWS * (q + 1)]
                        at = pl.multiple_of(HALF * h + QUART * q + c * CH, CH)
                        cols = pl.ds(at, CH)
                        both = jnp.concatenate([a, b], axis=0) * scale_v[:, cols]
                        dst = pl.ds(pl.multiple_of(k * 96 + 48 * pair, 48), 48)
                        scaled[h, dst, pl.ds(pl.multiple_of(QUART * q + c * CH, CH), CH)] = both.astype(bf16)
                        m = a * prod[rows_of(s0), cols] + b * prod[rows_of(s1), cols]
                        magacc[:, cols] += jnp.sum(m.reshape(ROWS // 8, 8, CH), axis=0)

    def multiply(h, first=0, last=F):
        for f in range(first, last, 256):
            w = min(256, F - f)
            r = dot(scaled[h], w_v[f : f + w, HALF * h : HALF * (h + 1)], 1, 1)
            for k in range(LINE):
                block = r[96 * k : 96 * (k + 1)]
                if h == 0:
                    at = pl.multiple_of(lax.rem(y + k + 3, LINE) * 96, 96)
                    hg[pl.ds(at, 96), f : f + w] = block
                else:
                    for yy in range(LINE):
                        s = yy * LINE + lax.rem(x + k + 3, LINE)
                        hg[rows_of(s), f : f + w] += block[ROWS * yy : ROWS * (yy + 1)]

    def send_mag():
        magp[...] = jnp.sum(magacc[...], axis=0, keepdims=True)
        magr[me_t] = magp[:, my_cols(me_t)]
        to_plane(M_RS, lambda p: magp.at[:, my_cols(p)], magr.at[me_t])

    def sum_mag_plane():
        got(M_RS, magr.at[fifteen])
        magd[me_d] = sum_of(magr, PEERS)
        to_group(M_DP, lambda p: magd.at[me_d], magd.at[me_d])

    def sum_mag_group():
        got(M_DP, magd.at[fifteen])
        gmag_v[:, my_cols(me_t)] = sum_of(magd, GROUP) / norm_v[:, my_cols(me_t)]
        to_plane(M_AG, lambda p: gmag_v.at[:, my_cols(me_t)], gmag_v.at[:, my_cols(me_t)])

    outs = [
        pltpu.make_async_copy(out_a, ggate_h, out_sem.at[0]),
        pltpu.make_async_copy(out_b, gup_h, out_sem.at[1]),
        pltpu.make_async_copy(gin_v, gin_h, out_sem.at[2]),
        pltpu.make_async_copy(gout_v, gout_h, out_sem.at[3]),
        pltpu.make_async_copy(gmag_v, gmag_h, out_sem.at[4]),
    ]

    def large_grads():
        @pl.loop(0, TOK // 16)
        def _(i):
            rows = pl.ds(pl.multiple_of(i * 16, 16), 16)
            g = hg[rows, :]
            out_b[rows, :] = (g * u_v[rows, :]).astype(bf16)
            out_a[rows, :] = (g * v_v[rows, :]).astype(bf16)

        outs[0].start()
        outs[1].start()

    def finish_in_grad():
        got(IN_AG, iag.at[fifteen])
        for b in range(4):
            for g in range(4):
                w = 256 if g < 3 else 128
                gin_v[16 * b : 16 * b + 16, 256 * g : 256 * g + w] = iag[4 * b + g, :, 0:w].astype(f32)
        outs[2].start()

    def finish_out_grad():
        other.wait_recv()
        for t in range(PEERS):
            for c in range(2):
                at = COLS * t + 128 * c
                gout_v[:, at : at + 128] = ob[c, t].astype(f32)
        outs[3].start()

    def finish_mag():
        got(M_AG, gmag_v.at[:, fifteen_cols])
        outs[4].start()

    start_adjust()
    adjust(0)

    pl.semaphore_wait(barrier, PEERS + GROUP - 2)
    for h in range(2):
        go(h, 0, 0, None, slot(h, 1, 0), 0)
        go(h, 0, 0, None, slot(h, -1, 0), 1)
    pl.loop(1, 5)(adjust)
    for h in range(2):
        send_across(h, 0)
    pl.loop(5, NWB)(adjust)
    send_squares()
    gate_and_up()
    project()
    pl.loop(0, 5)(produce)
    first_along()
    send_columns()
    pl.loop(5, 8)(produce)
    sum_squares()
    for h in range(2):
        forward_across(h, 0)
    sum_projected()
    last_along()
    pl.loop(8, 16)(produce)
    for h in range(2):
        forward_across(h, 1)
        forward_across(h, 2)
    column_scale()
    send_rank()
    out_grad()
    magacc[...] = jnp.zeros_like(magacc)
    prepare(1)
    for h in range(2):
        forward_across(h, 3)
    prepare(0)
    prepare(2)
    in_grad()
    for h in range(2):
        for j in range(4):
            last_across(h, j)
    prepare(3)
    send_mag()
    sum_out_grad()
    multiply(0)
    sum_mag_plane()
    spread_out_grad()
    sum_in_grad()
    multiply(1)
    large_grads()
    sum_mag_group()
    swap_out_grad()
    finish_in_grad()
    finish_out_grad()
    finish_mag()

    for c in sent:
        c.wait_send()
    other.wait_send()
    left_here(J, jsend.at[fifteen])
    left_here(SQ_RS, sqp.at[:, fifteen_cols])
    left_here(SQ_AG, sqf.at[:, fifteen_cols])
    left_here(PR_RS, prs.at[fifteen])
    left_here(PR_AG, pra.at[fifteen])
    left_here(RC_AG, rca.at[fifteen])
    left_here(IN_RS, ipart.at[fifteen])
    left_here(IN_AG, iag.at[fifteen])
    left_here(O_RS, opart.at[fifteen])
    left_here(O_PL, ob.at[0, fifteen])
    left_here(O_Z, oz.at[pl.ds(0, DEPTH - 1)])
    left_here(M_RS, magp.at[:, fifteen_cols])
    left_here(M_DP, magd.at[fifteen])
    left_here(M_AG, gmag_v.at[:, fifteen_cols])
    for c in outs:
        c.wait()


def hand_over(*refs):
    src, dst, held, sem_in, sem_out = refs[0:5], refs[5:10], refs[10:15], refs[15], refs[16]
    into = [pltpu.make_async_copy(src[i], held[i], sem_in.at[i]) for i in range(5)]
    out = [pltpu.make_async_copy(held[i], dst[i], sem_out.at[i]) for i in range(5)]
    for c in into:
        c.start()
    for i in range(5):
        into[i].wait()
        out[i].start()
    for c in out:
        c.wait()


def on_device(gate_act, up_act, cotangent, frozen_weight, adapter_in, adapter_out, magnitude):
    V = pltpu.VMEM
    scratch = [
        V((F, D), bf16), V((TOK, F), bf16), V((TOK, F), bf16), V((TOK, F), bf16),
        V((TOK, F), f32), V((TOK, F), f32), V((ROWS, D), bf16),
        V((2 * RANK, F), bf16), V((2 * RANK, D), bf16), V((1, D), f32), V((F, RANK), bf16),
        V((2, PEERS, 48, QUART), bf16), V((2, TOK, HALF), bf16), V((TOK, D), f32), V((TOK, F), f32),
        V((8, D), f32), V((8, D), f32), V((1, D), f32), V((1, D), f32),
        V((PEERS, 48, 128), bf16), V((PEERS, 48, 128), bf16), V((TOK, COLS), bf16),
        V((1, D), f32), V((PEERS, 1, COLS), f32), V((1, D), f32),
        V((PEERS, 16, 128), f32), V((PEERS, 16, 128), f32), V((PEERS, 16, 128), f32),
        V((16, 128), bf16), V((PEERS, 16, 128), bf16), V((TOK, 128), bf16),
        V((GROUP, 16, 256), bf16), V((GROUP, 16, 256), bf16), V((16, 256), bf16), V((GROUP, 16, 256), bf16),
        V((RANK, F), f32), V((GROUP, 8, 128), f32), V((GROUP, 8, 128), f32), V((DEPTH, 8, 128), f32),
        V((2, PEERS, RANK, 128), bf16), V((RANK, D), f32),
        V((1, D), f32), V((PEERS, 1, COLS), f32), V((GROUP, 1, COLS), f32), V((1, D), f32),
        V((TOK, F), bf16), V((TOK, F), bf16),
        pltpu.SemaphoreType.DMA((8,)), pltpu.SemaphoreType.DMA((NWB,)), pltpu.SemaphoreType.DMA((5,)),
        pltpu.SemaphoreType.DMA((N_PHASES,)), pltpu.SemaphoreType.DMA((N_PHASES,)),
        pltpu.SemaphoreType.DMA((40,)), pltpu.SemaphoreType.DMA((40,)),
    ]
    hbm = pl.BlockSpec(memory_space=pl.ANY)
    outs = pl.pallas_call(
        kernel,
        out_shape=(
            jax.ShapeDtypeStruct((TOK, F), bf16),
            jax.ShapeDtypeStruct((TOK, F), bf16),
            jax.ShapeDtypeStruct((RANK, F), f32),
            jax.ShapeDtypeStruct((RANK, D), f32),
            jax.ShapeDtypeStruct((1, D), f32),
        ),
        in_specs=[hbm] * 7,
        out_specs=[hbm] * 5,
        scratch_shapes=scratch,
        compiler_params=pltpu.CompilerParams(
            collective_id=0, has_side_effects=True, vmem_limit_bytes=60 * 1024 * 1024
        ),
        cost_estimate=pl.CostEstimate(flops=7_000_000_000, bytes_accessed=14_000_000, transcendentals=400_000),
    )(gate_act, up_act, cotangent, frozen_weight, adapter_in, adapter_out, magnitude.reshape(1, D))
    outs = pl.pallas_call(
        hand_over,
        out_shape=[jax.ShapeDtypeStruct(o.shape, o.dtype) for o in outs],
        in_specs=[hbm] * 5,
        out_specs=[hbm] * 5,
        scratch_shapes=[V(o.shape, o.dtype) for o in outs]
        + [pltpu.SemaphoreType.DMA((5,)), pltpu.SemaphoreType.DMA((5,))],
        compiler_params=pltpu.CompilerParams(vmem_limit_bytes=60 * 1024 * 1024),
    )(*outs)
    return outs[0], outs[1], outs[2], outs[3], outs[4].reshape(D)


def solution(mesh):
    in_specs = (
        P("dp", "tensor"),
        P("dp", "tensor"),
        P(("dp", "tensor"), None),
        P("tensor", None),
        P(None, "tensor"),
        P(),
        P(),
    )
    out_specs = (P("dp", "tensor"), P("dp", "tensor"), P(None, "tensor"), P(), P())
    return jax.shard_map(
        on_device, mesh=mesh, in_specs=in_specs, out_specs=out_specs, check_vma=False
    )
```

```python
import jax
import jax.numpy as jnp
from jax import lax
from jax.experimental import pallas as pl
from jax.experimental.pallas import tpu as pltpu
from jax.sharding import PartitionSpec as P

epsilon = 1e-06
MESH = pl.DeviceIdType.MESH
f32 = jnp.float32
bf16 = jnp.bfloat16

LINE = 4
PEERS = LINE * LINE
GROUP = 16
DEPTH = GROUP // 2
ROWS = 24
TOK = ROWS * PEERS
F = 896
D = 4096
RANK = 64
HALF = D // 2
QUART = D // 4
COLS = D // PEERS
WBLK = 128
NWB = F // WBLK

(J, SQ_RS, SQ_AG, PR_RS, PR_AG, RC_AG, IN_RS, IN_AG, O_RS, O_PL, O_Z, O_CORE, M_RS, M_DP, M_AG) = range(15)
N_PHASES = 15


def dot(a, b, da, db):
    return lax.dot_general(a, b, (((da,), (db,)), ((), ())), preferred_element_type=f32)


def kernel(
    gate_h, up_h, cot_h, w_h, ain_h, aout_h, mag_h,
    ggate_h, gup_h, gin_h, gout_h, gmag_h,
    w_v, gate_v, up_v, hid_v, u_v, v_v, cot_v, ain_v, aout_v, mag_v, aint_v,
    cotb, scaled, prod, hg, magacc, scale_v, norm_v,
    jsend, jrecv, wj_v, sqr, sqf, prs, prr, pra, rcs, rca, lv,
    ipart, irecv, isum, iag, gin_v, opart, orecv, oz, ob, gout_v,
    magp, magr, magd, gmag_v, out_a, out_b,
    loc_sem, w_sem, out_sem, ph_send, ph_recv, g_send, g_recv,
):
    me_t = lax.axis_index("tensor")
    me_d = lax.axis_index("dp")
    x = lax.rem(me_t, LINE)
    y = lax.div(me_t, LINE)
    z = lax.div(me_d, 2)
    core = lax.rem(me_d, 2)

    loads = [
        pltpu.make_async_copy(cot_h, cot_v, loc_sem.at[0]),
        pltpu.make_async_copy(ain_h, ain_v.at[pl.ds(0, RANK)], loc_sem.at[1]),
        pltpu.make_async_copy(aout_h, aout_v.at[pl.ds(0, RANK)], loc_sem.at[2]),
        pltpu.make_async_copy(gate_h, gate_v, loc_sem.at[3]),
        pltpu.make_async_copy(up_h, up_v, loc_sem.at[4]),
        pltpu.make_async_copy(ain_h, ain_v.at[pl.ds(RANK, RANK)], loc_sem.at[5]),
        pltpu.make_async_copy(aout_h, aout_v.at[pl.ds(RANK, RANK)], loc_sem.at[6]),
        pltpu.make_async_copy(mag_h, mag_v, loc_sem.at[7]),
    ]

    def w_copy(i):
        rows = pl.ds(pl.multiple_of(i * WBLK, WBLK), WBLK)
        return pltpu.make_async_copy(w_h.at[rows], w_v.at[rows], w_sem.at[i])

    my_part = pl.ds(pl.multiple_of(me_d * COLS, COLS), COLS)
    wj_copy = pltpu.make_async_copy(w_h.at[:, my_part], wj_v, loc_sem.at[8])
    for c in loads[0:3]:
        c.start()
    wj_copy.start()
    for c in loads[3:6]:
        c.start()
    for i in range(NWB):
        w_copy(i).start()
    for c in loads[6:]:
        c.start()

    barrier = pltpu.get_barrier_semaphore()

    @pl.loop(1, PEERS)
    def _(d):
        pl.semaphore_signal(barrier, inc=1, device_id={"tensor": lax.rem(me_t + d, PEERS)}, device_id_type=MESH)

    @pl.loop(1, GROUP)
    def _(d):
        pl.semaphore_signal(barrier, inc=1, device_id={"dp": lax.rem(me_d + d, GROUP)}, device_id_type=MESH)

    loads[0].wait()
    for h in range(2):
        left = cot_v[:, HALF * h : HALF * h + QUART].astype(f32)
        right = cot_v[:, HALF * h + QUART : HALF * (h + 1)].astype(f32)
        cotb[h, me_t] = jnp.concatenate([left, right], axis=0).astype(bf16)

    def slot(h, along, across):
        if h == 0:
            return lax.rem(y + across + LINE, LINE) * LINE + lax.rem(x + along + LINE, LINE)
        return lax.rem(y + along + LINE, LINE) * LINE + lax.rem(x + across + LINE, LINE)

    def move(h, along, across, part, to, sem):
        if part is None:
            ref = cotb.at[h, slot(h, along, across)]
        else:
            ref = cotb.at[h, slot(h, along, across), :, pl.ds(part * (QUART // 2), QUART // 2)]
        return pltpu.make_async_remote_copy(
            src_ref=ref, dst_ref=ref, send_sem=g_send.at[20 * h + sem], recv_sem=g_recv.at[20 * h + sem],
            device_id={"tensor": to}, device_id_type=MESH,
        )

    sent = []

    def go(h, along, across, part, to, sem):
        c = move(h, along, across, part, to, sem)
        c.start()
        sent.append(c)

    def arrive(h, along, across, part, sem):
        move(h, along, across, part, slot(h, 0, 1), sem).wait_recv()

    offsets = (0, -1, 1, 2)

    def send_across(h, j):
        go(h, offsets[j], 0, None, slot(h, 0, 1), 4 + 4 * j)
        go(h, offsets[j], 0, None, slot(h, 0, -1), 5 + 4 * j)

    def forward_across(h, j):
        arrive(h, offsets[j], -1, None, 4 + 4 * j)
        go(h, offsets[j], -1, 0, slot(h, 0, 1), 6 + 4 * j)
        arrive(h, offsets[j], 1, None, 5 + 4 * j)
        go(h, offsets[j], 1, 1, slot(h, 0, -1), 7 + 4 * j)

    def last_across(h, j):
        arrive(h, offsets[j], 2, 0, 6 + 4 * j)
        arrive(h, offsets[j], 2, 1, 7 + 4 * j)

    def exchange(phase, axis, src, dst, me, n):
        def one(p):
            return pltpu.make_async_remote_copy(
                src_ref=src(p), dst_ref=dst, send_sem=ph_send.at[phase], recv_sem=ph_recv.at[phase],
                device_id={axis: p}, device_id_type=MESH,
            )

        @pl.loop(1, n)
        def _(d):
            one(lax.rem(me + d, n)).start()

    def got(phase, ref):
        pltpu.make_async_copy(ref, ref, ph_recv.at[phase]).wait()

    def left_here(phase, ref):
        pltpu.make_async_copy(ref, ref, ph_send.at[phase]).wait()

    def to_plane(phase, src, dst):
        exchange(phase, "tensor", src, dst, me_t, PEERS)

    def to_group(phase, src, dst):
        exchange(phase, "dp", src, dst, me_d, GROUP)

    def my_cols(p):
        return pl.ds(pl.multiple_of(p * COLS, COLS), COLS)

    fifteen = pl.ds(0, 15)
    fifteen_cols = pl.ds(0, 15 * COLS)

    def sum_of(ref, n):
        total = ref[0]
        for t in range(1, n):
            total = total + ref[t]
        return total

    low_lanes = lax.broadcasted_iota(jnp.int32, (8, 128), 1) < RANK

    def gate_and_up():
        loads[3].wait()
        loads[4].wait()

        @pl.loop(0, TOK // 16)
        def _(i):
            rows = pl.ds(pl.multiple_of(i * 16, 16), 16)
            g = gate_v[rows, :].astype(f32)
            u = up_v[rows, :].astype(f32)
            s = 1.0 / (1.0 + jnp.exp(-g))
            gs = g * s
            hid_v[rows, :] = (gs * u).astype(bf16)
            u_v[rows, :] = gs
            v_v[rows, :] = u * s * (1.0 + g * (1.0 - s))

    def project():
        loads[5].wait()
        part = dot(hid_v[...], ain_v[...], 1, 1)
        for t in range(PEERS):
            r = ROWS * t
            prs[t, 0:8] = jnp.where(low_lanes, part[r : r + 8], part[r + 8 : r + 16])
            prs[t, 8:16] = part[r + 16 : r + 24]
        prr[me_t] = prs[me_t]
        to_plane(PR_RS, lambda p: prs.at[p], prr.at[me_t])

    def square_part():
        loads[1].wait()
        aint_v[...] = (2.0 * jnp.transpose(ain_v[0:RANK, :].astype(f32), (1, 0))).astype(bf16)
        loads[2].wait()
        wj_copy.wait()
        squares = jnp.zeros((8, COLS), f32)
        for i in range(NWB):
            rows = slice(WBLK * i, WBLK * (i + 1))
            a = wj_v[rows, :].astype(f32) + dot(aint_v[rows, :], aout_v[0:RANK, my_part], 1, 0)
            squares = squares + jnp.sum((a * a).reshape(WBLK // 8, 8, COLS), axis=0)
        sqr[me_t] = jnp.sum(squares, axis=0, keepdims=True)

    def send_squares():
        to_plane(SQ_RS, lambda p: sqr.at[me_t], sqr.at[me_t])

    def sum_squares():
        got(SQ_RS, sqr.at[fifteen])
        sqf[:, my_part] = sum_of(sqr, PEERS)
        to_group(SQ_AG, lambda p: sqf.at[:, my_part], sqf.at[:, my_part])

    def adjust(i):
        w_copy(i).wait()
        rows = pl.ds(pl.multiple_of(i * WBLK, WBLK), WBLK)
        lhs = aint_v[rows, :]
        for c in range(8):
            cols = slice(512 * c, 512 * (c + 1))
            a = w_v[rows, cols].astype(f32) + dot(lhs, aout_v[0:RANK, cols], 1, 0)
            w_v[rows, cols] = a.astype(bf16)

    def send_columns():
        for h in range(2):
            for d in range(LINE):
                to = slot(h, 0, d)
                low = to < PEERS // 2
                at = pl.ds(pl.multiple_of(lax.rem(to, PEERS // 2) * 128, 128), 128)
                rows = []
                for m in range(LINE):
                    c = cotb[h, y * LINE + m if h == 0 else m * LINE + x, :, at].astype(f32)
                    rows.append(jnp.where(low, c[0:ROWS], c[ROWS : 2 * ROWS]))
                jsend[h, d] = jnp.concatenate(rows, axis=0).astype(bf16)
        for h in range(2):
            me = y if h == 0 else x
            jrecv[h, me] = jsend[h, 0]
            for d in range(1, LINE):
                pltpu.make_async_remote_copy(
                    src_ref=jsend.at[h, d], dst_ref=jrecv.at[h, me], send_sem=ph_send.at[J], recv_sem=ph_recv.at[J],
                    device_id={"tensor": slot(h, 0, d)}, device_id_type=MESH,
                ).start()

    def first_along():
        for h in range(2):
            arrive(h, -1, 0, None, 0)
            go(h, -1, 0, 0, slot(h, 1, 0), 2)
            arrive(h, 1, 0, None, 1)
            go(h, 1, 0, 1, slot(h, -1, 0), 3)

    def last_along():
        for h in range(2):
            arrive(h, 2, 0, 0, 2)
            arrive(h, 2, 0, 1, 3)

    def sum_projected():
        got(PR_RS, prr.at[fifteen])
        pra[me_t] = sum_of(prr, PEERS)
        to_plane(PR_AG, lambda p: pra.at[me_t], pra.at[me_t])

    def produce(i):
        cols = pl.ds(pl.multiple_of(i * 256, 256), 256)
        prod[:, cols] = dot(hid_v[...], w_v[:, cols], 1, 0)

    def out_grad():
        got(J, jrecv.at[:, pl.ds(0, LINE - 1)])
        got(PR_AG, pra.at[fifteen])
        lanes = lax.broadcasted_iota(jnp.int32, (2 * ROWS, 128), 1) < RANK
        o = []
        for h in range(2):
            for i in range(0, PEERS, 2):

                def three(n):
                    t = n if h == 0 else n % LINE * LINE + n // LINE
                    tile = pra[t, 0:8]
                    turned = pltpu.roll(tile, RANK, 1)
                    return [jnp.where(low_lanes, tile, turned), jnp.where(low_lanes, turned, tile), pra[t, 8:16]]

                rows = jnp.concatenate(three(i) + three(i + 1), axis=0)
                high = rows.astype(bf16).astype(f32)
                lv[ROWS * i : ROWS * (i + 2), :] = jnp.where(lanes, high, rows - high).astype(bf16)
            both = dot(lv[...], jrecv[h].reshape(TOK, 128), 0, 0)
            o.append(both[0:RANK] + both[RANK:])
        for p in range(GROUP):
            opart[p] = o[p % 2][8 * (p // 2) : 8 * (p // 2) + 8]
        orecv[me_d] = opart[me_d]
        to_group(O_RS, lambda p: opart.at[p], orecv.at[me_d])

    def sum_out_grad():
        got(O_RS, orecv.at[fifteen])
        mine = pl.ds(pl.multiple_of(core * HALF + me_t * 128, 128), 128)
        oz[z] = 2.0 * sum_of(orecv, GROUP) * scale_v[:, mine]

        @pl.loop(1, DEPTH)
        def _(d):
            pltpu.make_async_remote_copy(
                src_ref=oz.at[z], dst_ref=oz.at[z], send_sem=ph_send.at[O_Z], recv_sem=ph_recv.at[O_Z],
                device_id={"dp": lax.rem(z + d, DEPTH) * 2 + core}, device_id_type=MESH,
            ).start()

    def spread_out_grad():
        got(O_Z, oz.at[pl.ds(0, DEPTH - 1)])
        ob[core, me_t] = oz[...].reshape(RANK, 128).astype(bf16)
        to_plane(O_PL, lambda p: ob.at[core, me_t], ob.at[core, me_t])

    other = pltpu.make_async_remote_copy(
        src_ref=ob.at[core], dst_ref=ob.at[core], send_sem=ph_send.at[O_CORE], recv_sem=ph_recv.at[O_CORE],
        device_id={"dp": z * 2 + 1 - core}, device_id_type=MESH,
    )

    def swap_out_grad():
        got(O_PL, ob.at[0, fifteen])
        other.start()

    def column_scale():
        loads[7].wait()
        got(SQ_AG, sqf.at[:, fifteen_cols])
        norm_v[...] = jnp.sqrt(sqf[...] + epsilon)
        scale_v[...] = mag_v[...] / norm_v[...]

    def send_rank():
        loads[6].wait()
        rank = jnp.zeros((32, 128), f32)
        for c in range(8):
            cols = slice(512 * c, 512 * (c + 1))
            s = cot_v[:, cols].astype(f32) * scale_v[:, cols]
            s = jnp.concatenate([s, jnp.zeros((8, 512), f32)], axis=0).astype(bf16)
            rank = rank + dot(s, aout_v[:, cols], 1, 1)
        rcs[...] = jnp.concatenate([jnp.where(low_lanes, rank[0:8], rank[8:16]), rank[16:24]], axis=0).astype(bf16)
        rca[me_t] = rcs[...]
        to_plane(RC_AG, lambda p: rcs, rca.at[me_t])

    def in_grad():
        got(RC_AG, rca.at[fifteen])
        for t in range(0, PEERS, 2):
            c0 = rca[t].astype(f32)
            c1 = rca[t + 1].astype(f32)
            rows = jnp.concatenate(
                [c0[0:8], pltpu.roll(c0[0:8], RANK, 1), c0[8:16], c1[0:8], pltpu.roll(c1[0:8], RANK, 1), c1[8:16]], axis=0
            )
            lv[ROWS * t : ROWS * (t + 2), :] = rows.astype(bf16)
        for g in range(4):
            w = 256 if g < 3 else 128
            o = dot(lv[...], hid_v[:, 256 * g : 256 * g + w], 0, 0).astype(bf16)
            for b in range(4):
                ipart[4 * b + g, :, 0:w] = o[16 * b : 16 * b + 16]
                if w < 256:
                    ipart[4 * b + g, :, w:256] = jnp.zeros((16, 256 - w), bf16)
        irecv[me_d] = ipart[me_d]
        to_group(IN_RS, lambda p: ipart.at[p], irecv.at[me_d])

    def sum_in_grad():
        got(IN_RS, irecv.at[fifteen])
        total = irecv[0].astype(f32)
        for t in range(1, GROUP):
            total = total + irecv[t].astype(f32)
        isum[...] = (2.0 * total).astype(bf16)
        iag[me_d] = isum[...]
        to_group(IN_AG, lambda p: isum, iag.at[me_d])

    CH = 256

    def rows_of(s):
        return pl.ds(pl.multiple_of(s * ROWS, ROWS), ROWS)

    def prepare(k):
        for h in range(2):
            for pair in range(2):
                if h == 0:
                    s0 = lax.rem(y + k + 3, LINE) * LINE + 2 * pair
                    s1 = s0 + 1
                else:
                    s0 = 2 * pair * LINE + lax.rem(x + k + 3, LINE)
                    s1 = s0 + LINE

                @pl.loop(0, QUART // CH)
                def _(c):
                    here = pl.ds(pl.multiple_of(c * CH, CH), CH)
                    c0 = cotb[h, s0, :, here].astype(f32)
                    c1 = cotb[h, s1, :, here].astype(f32)
                    for q in range(2):
                        a = c0[ROWS * q : ROWS * (q + 1)]
                        b = c1[ROWS * q : ROWS * (q + 1)]
                        at = pl.multiple_of(HALF * h + QUART * q + c * CH, CH)
                        cols = pl.ds(at, CH)
                        both = jnp.concatenate([a, b], axis=0) * scale_v[:, cols]
                        dst = pl.ds(pl.multiple_of(k * 96 + 48 * pair, 48), 48)
                        scaled[h, dst, pl.ds(pl.multiple_of(QUART * q + c * CH, CH), CH)] = both.astype(bf16)
                        m = a * prod[rows_of(s0), cols] + b * prod[rows_of(s1), cols]
                        magacc[:, cols] += jnp.sum(m.reshape(ROWS // 8, 8, CH), axis=0)

    def multiply(h, first=0, last=F):
        for f in range(first, last, 256):
            w = min(256, F - f)
            r = dot(scaled[h], w_v[f : f + w, HALF * h : HALF * (h + 1)], 1, 1)
            for k in range(LINE):
                block = r[96 * k : 96 * (k + 1)]
                if h == 0:
                    at = pl.multiple_of(lax.rem(y + k + 3, LINE) * 96, 96)
                    hg[pl.ds(at, 96), f : f + w] = block
                else:
                    for yy in range(LINE):
                        s = yy * LINE + lax.rem(x + k + 3, LINE)
                        hg[rows_of(s), f : f + w] += block[ROWS * yy : ROWS * (yy + 1)]

    def send_mag():
        magp[...] = jnp.sum(magacc[...], axis=0, keepdims=True)
        magr[me_t] = magp[:, my_cols(me_t)]
        to_plane(M_RS, lambda p: magp.at[:, my_cols(p)], magr.at[me_t])

    def sum_mag_plane():
        got(M_RS, magr.at[fifteen])
        magd[me_d] = sum_of(magr, PEERS)
        to_group(M_DP, lambda p: magd.at[me_d], magd.at[me_d])

    def sum_mag_group():
        got(M_DP, magd.at[fifteen])
        gmag_v[:, my_cols(me_t)] = sum_of(magd, GROUP) / norm_v[:, my_cols(me_t)]
        to_plane(M_AG, lambda p: gmag_v.at[:, my_cols(me_t)], gmag_v.at[:, my_cols(me_t)])

    outs = [
        pltpu.make_async_copy(out_a, ggate_h, out_sem.at[0]),
        pltpu.make_async_copy(out_b, gup_h, out_sem.at[1]),
        pltpu.make_async_copy(gin_v, gin_h, out_sem.at[2]),
        pltpu.make_async_copy(gout_v, gout_h, out_sem.at[3]),
        pltpu.make_async_copy(gmag_v, gmag_h, out_sem.at[4]),
    ]

    def large_grads():
        @pl.loop(0, TOK // 16)
        def _(i):
            rows = pl.ds(pl.multiple_of(i * 16, 16), 16)
            g = hg[rows, :]
            out_b[rows, :] = (g * u_v[rows, :]).astype(bf16)
            out_a[rows, :] = (g * v_v[rows, :]).astype(bf16)

        outs[0].start()
        outs[1].start()

    def finish_in_grad():
        got(IN_AG, iag.at[fifteen])
        for b in range(4):
            for g in range(4):
                w = 256 if g < 3 else 128
                gin_v[16 * b : 16 * b + 16, 256 * g : 256 * g + w] = iag[4 * b + g, :, 0:w].astype(f32)
        outs[2].start()

    def finish_out_grad():
        other.wait_recv()
        for t in range(PEERS):
            for c in range(2):
                at = HALF * c + 128 * t
                gout_v[:, at : at + 128] = ob[c, t].astype(f32)
        outs[3].start()

    def finish_mag():
        got(M_AG, gmag_v.at[:, fifteen_cols])
        outs[4].start()

    pl.semaphore_wait(barrier, PEERS + GROUP - 2)
    for h in range(2):
        go(h, 0, 0, None, slot(h, 1, 0), 0)
        go(h, 0, 0, None, slot(h, -1, 0), 1)
    square_part()
    send_squares()
    gate_and_up()
    project()
    for h in range(2):
        send_across(h, 0)
    pl.loop(0, NWB)(adjust)
    first_along()
    for h in range(2):
        send_across(h, 1)
    pl.loop(0, 5)(produce)
    sum_squares()
    sum_projected()
    for h in range(2):
        send_across(h, 2)
    pl.loop(5, 10)(produce)
    last_along()
    send_columns()
    for h in range(2):
        send_across(h, 3)
    for h in range(2):
        forward_across(h, 0)
    pl.loop(10, 16)(produce)
    column_scale()
    send_rank()
    for h in range(2):
        forward_across(h, 1)
        forward_across(h, 2)
    magacc[...] = jnp.zeros_like(magacc)
    prepare(1)
    out_grad()
    for h in range(2):
        forward_across(h, 3)
    prepare(0)
    prepare(2)
    in_grad()
    for h in range(2):
        for j in range(4):
            last_across(h, j)
    prepare(3)
    send_mag()
    multiply(0)
    sum_out_grad()
    multiply(1, 0, 512)
    sum_mag_plane()
    sum_in_grad()
    multiply(1, 512, F)
    spread_out_grad()
    large_grads()
    sum_mag_group()
    swap_out_grad()
    finish_in_grad()
    finish_out_grad()
    finish_mag()

    for c in sent:
        c.wait_send()
    other.wait_send()
    left_here(J, jsend.at[:, pl.ds(0, LINE - 1)])
    left_here(SQ_RS, sqr.at[fifteen])
    left_here(SQ_AG, sqf.at[:, fifteen_cols])
    left_here(PR_RS, prs.at[fifteen])
    left_here(PR_AG, pra.at[fifteen])
    left_here(RC_AG, rca.at[fifteen])
    left_here(IN_RS, ipart.at[fifteen])
    left_here(IN_AG, iag.at[fifteen])
    left_here(O_RS, opart.at[fifteen])
    left_here(O_PL, ob.at[0, fifteen])
    left_here(O_Z, oz.at[pl.ds(0, DEPTH - 1)])
    left_here(M_RS, magp.at[:, fifteen_cols])
    left_here(M_DP, magd.at[fifteen])
    left_here(M_AG, gmag_v.at[:, fifteen_cols])
    for c in outs:
        c.wait()


def hand_over(*refs):
    src, dst, held, sem_in, sem_out = refs[0:5], refs[5:10], refs[10:15], refs[15], refs[16]
    into = [pltpu.make_async_copy(src[i], held[i], sem_in.at[i]) for i in range(5)]
    out = [pltpu.make_async_copy(held[i], dst[i], sem_out.at[i]) for i in range(5)]
    for c in into:
        c.start()
    for i in range(5):
        into[i].wait()
        out[i].start()
    for c in out:
        c.wait()


def on_device(gate_act, up_act, cotangent, frozen_weight, adapter_in, adapter_out, magnitude):
    V = pltpu.VMEM
    scratch = [
        V((F, D), bf16), V((TOK, F), bf16), V((TOK, F), bf16), V((TOK, F), bf16),
        V((TOK, F), f32), V((TOK, F), f32), V((ROWS, D), bf16),
        V((2 * RANK, F), bf16), V((2 * RANK, D), bf16), V((1, D), f32), V((F, RANK), bf16),
        V((2, PEERS, 48, QUART), bf16), V((2, TOK, HALF), bf16), V((TOK, D), f32), V((TOK, F), f32),
        V((8, D), f32), V((1, D), f32), V((1, D), f32),
        V((2, LINE, 96, 128), bf16), V((2, LINE, 96, 128), bf16),
        V((F, COLS), bf16), V((PEERS, 1, COLS), f32), V((1, D), f32),
        V((PEERS, 16, 128), f32), V((PEERS, 16, 128), f32), V((PEERS, 16, 128), f32),
        V((16, 128), bf16), V((PEERS, 16, 128), bf16), V((TOK, 128), bf16),
        V((GROUP, 16, 256), bf16), V((GROUP, 16, 256), bf16), V((16, 256), bf16), V((GROUP, 16, 256), bf16),
        V((RANK, F), f32), V((GROUP, 8, 128), f32), V((GROUP, 8, 128), f32), V((DEPTH, 8, 128), f32),
        V((2, PEERS, RANK, 128), bf16), V((RANK, D), f32),
        V((1, D), f32), V((PEERS, 1, COLS), f32), V((GROUP, 1, COLS), f32), V((1, D), f32),
        V((TOK, F), bf16), V((TOK, F), bf16),
        pltpu.SemaphoreType.DMA((9,)), pltpu.SemaphoreType.DMA((NWB,)), pltpu.SemaphoreType.DMA((5,)),
        pltpu.SemaphoreType.DMA((N_PHASES,)), pltpu.SemaphoreType.DMA((N_PHASES,)),
        pltpu.SemaphoreType.DMA((40,)), pltpu.SemaphoreType.DMA((40,)),
    ]
    hbm = pl.BlockSpec(memory_space=pl.ANY)
    outs = pl.pallas_call(
        kernel,
        out_shape=(
            jax.ShapeDtypeStruct((TOK, F), bf16),
            jax.ShapeDtypeStruct((TOK, F), bf16),
            jax.ShapeDtypeStruct((RANK, F), f32),
            jax.ShapeDtypeStruct((RANK, D), f32),
            jax.ShapeDtypeStruct((1, D), f32),
        ),
        in_specs=[hbm] * 7,
        out_specs=[hbm] * 5,
        scratch_shapes=scratch,
        compiler_params=pltpu.CompilerParams(
            collective_id=0, has_side_effects=True, vmem_limit_bytes=60 * 1024 * 1024
        ),
        cost_estimate=pl.CostEstimate(flops=7_000_000_000, bytes_accessed=14_000_000, transcendentals=400_000),
    )(gate_act, up_act, cotangent, frozen_weight, adapter_in, adapter_out, magnitude.reshape(1, D))
    outs = pl.pallas_call(
        hand_over,
        out_shape=[jax.ShapeDtypeStruct(o.shape, o.dtype) for o in outs],
        in_specs=[hbm] * 5,
        out_specs=[hbm] * 5,
        scratch_shapes=[V(o.shape, o.dtype) for o in outs]
        + [pltpu.SemaphoreType.DMA((5,)), pltpu.SemaphoreType.DMA((5,))],
        compiler_params=pltpu.CompilerParams(vmem_limit_bytes=60 * 1024 * 1024),
    )(*outs)
    return outs[0], outs[1], outs[2], outs[3], outs[4].reshape(D)


def solution(mesh):
    in_specs = (
        P("dp", "tensor"),
        P("dp", "tensor"),
        P(("dp", "tensor"), None),
        P("tensor", None),
        P(None, "tensor"),
        P(),
        P(),
    )
    out_specs = (P("dp", "tensor"), P("dp", "tensor"), P(None, "tensor"), P(), P())
    return jax.shard_map(
        on_device, mesh=mesh, in_specs=in_specs, out_specs=out_specs, check_vma=False
    )
```

```python
import jax
import jax.numpy as jnp
from jax import lax
from jax.experimental import pallas as pl
from jax.experimental.pallas import tpu as pltpu
from jax.sharding import PartitionSpec as P

epsilon = 1e-06
MESH = pl.DeviceIdType.MESH
f32 = jnp.float32
bf16 = jnp.bfloat16

LINE = 4
PEERS = LINE * LINE
GROUP = 16
DEPTH = GROUP // 2
ROWS = 24
TOK = ROWS * PEERS
F = 896
D = 4096
RANK = 64
HALF = D // 2
QUART = D // 4
COLS = D // PEERS
WBLK = 128
NWB = F // WBLK

(J, SQ_RS, SQ_AG, PR_RS, PR_AG, RC_AG, IN_RS, IN_AG, O_RS, O_PL, O_Z, O_CORE, M_RS, M_DP, M_AG, IN_CORE) = range(16)
N_PHASES = 16


def dot(a, b, da, db):
    return lax.dot_general(a, b, (((da,), (db,)), ((), ())), preferred_element_type=f32)


def kernel(
    gate_h, up_h, cot_h, w_h, ain_h, aout_h, mag_h,
    ggate_h, gup_h, gin_h, gout_h, gmag_h,
    w_v, gate_v, up_v, hid_v, u_v, v_v, cot_v, ain_v, aout_v, mag_v, aint_v,
    cotb, scaled, prod, hg, magacc, scale_v, norm_v,
    jsend, jrecv, wj_v, sqr, sqf, prs, prr, pra, rcs, rca, lv,
    ipart, irecv, iag, gin_v, opart, orecv, oz, ob, gout_v,
    magp, magr, magd, gmag_v, out_a, out_b,
    loc_sem, w_sem, out_sem, ph_send, ph_recv, g_send, g_recv,
):
    me_t = lax.axis_index("tensor")
    me_d = lax.axis_index("dp")
    x = lax.rem(me_t, LINE)
    y = lax.div(me_t, LINE)
    z = lax.div(me_d, 2)
    core = lax.rem(me_d, 2)

    barrier = pltpu.get_barrier_semaphore()

    @pl.loop(1, PEERS)
    def _(d):
        pl.semaphore_signal(barrier, inc=1, device_id={"tensor": lax.rem(me_t + d, PEERS)}, device_id_type=MESH)

    @pl.loop(1, GROUP)
    def _(d):
        pl.semaphore_signal(barrier, inc=1, device_id={"dp": lax.rem(me_d + d, GROUP)}, device_id_type=MESH)

    loads = [
        pltpu.make_async_copy(cot_h, cot_v, loc_sem.at[0]),
        pltpu.make_async_copy(ain_h, ain_v.at[pl.ds(0, RANK)], loc_sem.at[1]),
        pltpu.make_async_copy(aout_h, aout_v.at[pl.ds(0, RANK)], loc_sem.at[2]),
        pltpu.make_async_copy(gate_h, gate_v, loc_sem.at[3]),
        pltpu.make_async_copy(up_h, up_v, loc_sem.at[4]),
        pltpu.make_async_copy(ain_h, ain_v.at[pl.ds(RANK, RANK)], loc_sem.at[5]),
        pltpu.make_async_copy(aout_h, aout_v.at[pl.ds(RANK, RANK)], loc_sem.at[6]),
        pltpu.make_async_copy(mag_h, mag_v, loc_sem.at[7]),
    ]

    def w_copy(i):
        rows = pl.ds(pl.multiple_of(i * WBLK, WBLK), WBLK)
        return pltpu.make_async_copy(w_h.at[rows], w_v.at[rows], w_sem.at[i])

    my_part = pl.ds(pl.multiple_of(me_d * COLS, COLS), COLS)
    wj_copy = pltpu.make_async_copy(w_h.at[:, my_part], wj_v, loc_sem.at[8])
    for c in loads[0:3]:
        c.start()
    wj_copy.start()
    for c in loads[3:6]:
        c.start()
    for i in range(NWB):
        w_copy(i).start()
    for c in loads[6:]:
        c.start()

    loads[0].wait()
    for h in range(2):
        left = cot_v[:, HALF * h : HALF * h + QUART].astype(f32)
        right = cot_v[:, HALF * h + QUART : HALF * (h + 1)].astype(f32)
        cotb[h, me_t] = jnp.concatenate([left, right], axis=0).astype(bf16)

    def slot(h, along, across):
        if h == 0:
            return lax.rem(y + across + LINE, LINE) * LINE + lax.rem(x + along + LINE, LINE)
        return lax.rem(y + along + LINE, LINE) * LINE + lax.rem(x + across + LINE, LINE)

    def move(h, along, across, part, to, sem):
        if part is None:
            ref = cotb.at[h, slot(h, along, across)]
        else:
            ref = cotb.at[h, slot(h, along, across), :, pl.ds(part * (QUART // 2), QUART // 2)]
        return pltpu.make_async_remote_copy(
            src_ref=ref, dst_ref=ref, send_sem=g_send.at[20 * h + sem], recv_sem=g_recv.at[20 * h + sem],
            device_id={"tensor": to}, device_id_type=MESH,
        )

    sent = []

    def go(h, along, across, part, to, sem):
        c = move(h, along, across, part, to, sem)
        c.start()
        sent.append(c)

    def arrive(h, along, across, part, sem):
        move(h, along, across, part, slot(h, 0, 1), sem).wait_recv()

    offsets = (0, -1, 1, 2)

    def send_across(h, j):
        go(h, offsets[j], 0, None, slot(h, 0, 1), 4 + 4 * j)
        go(h, offsets[j], 0, None, slot(h, 0, -1), 5 + 4 * j)

    def forward_across(h, j):
        arrive(h, offsets[j], -1, None, 4 + 4 * j)
        go(h, offsets[j], -1, 0, slot(h, 0, 1), 6 + 4 * j)
        arrive(h, offsets[j], 1, None, 5 + 4 * j)
        go(h, offsets[j], 1, 1, slot(h, 0, -1), 7 + 4 * j)

    def last_across(h, j):
        arrive(h, offsets[j], 2, 0, 6 + 4 * j)
        arrive(h, offsets[j], 2, 1, 7 + 4 * j)

    def exchange(phase, axis, src, dst, me, n):
        def one(p):
            return pltpu.make_async_remote_copy(
                src_ref=src(p), dst_ref=dst, send_sem=ph_send.at[phase], recv_sem=ph_recv.at[phase],
                device_id={axis: p}, device_id_type=MESH,
            )

        @pl.loop(1, n)
        def _(d):
            one(lax.rem(me + d, n)).start()

    def got(phase, ref):
        pltpu.make_async_copy(ref, ref, ph_recv.at[phase]).wait()

    def left_here(phase, ref):
        pltpu.make_async_copy(ref, ref, ph_send.at[phase]).wait()

    def to_plane(phase, src, dst):
        exchange(phase, "tensor", src, dst, me_t, PEERS)

    def to_group(phase, src, dst):
        exchange(phase, "dp", src, dst, me_d, GROUP)

    def along_z(phase, ref):
        @pl.loop(1, DEPTH)
        def _(d):
            pltpu.make_async_remote_copy(
                src_ref=ref, dst_ref=ref, send_sem=ph_send.at[phase], recv_sem=ph_recv.at[phase],
                device_id={"dp": lax.rem(z + d, DEPTH) * 2 + core}, device_id_type=MESH,
            ).start()

    def swap(phase, ref):
        return pltpu.make_async_remote_copy(
            src_ref=ref, dst_ref=ref, send_sem=ph_send.at[phase], recv_sem=ph_recv.at[phase],
            device_id={"dp": z * 2 + 1 - core}, device_id_type=MESH,
        )

    def my_cols(p):
        return pl.ds(pl.multiple_of(p * COLS, COLS), COLS)

    fifteen = pl.ds(0, 15)
    fifteen_cols = pl.ds(0, 15 * COLS)

    def sum_of(ref, n):
        total = ref[0]
        for t in range(1, n):
            total = total + ref[t]
        return total

    low_lanes = lax.broadcasted_iota(jnp.int32, (8, 128), 1) < RANK

    def gate_and_up():
        loads[3].wait()
        loads[4].wait()

        @pl.loop(0, TOK // 16)
        def _(i):
            rows = pl.ds(pl.multiple_of(i * 16, 16), 16)
            g = gate_v[rows, :].astype(f32)
            u = up_v[rows, :].astype(f32)
            s = 1.0 / (1.0 + jnp.exp(-g))
            gs = g * s
            hid_v[rows, :] = (gs * u).astype(bf16)
            u_v[rows, :] = gs
            v_v[rows, :] = u * s * (1.0 + g * (1.0 - s))

    def project():
        loads[5].wait()
        part = dot(hid_v[...], ain_v[...], 1, 1)
        for t in range(PEERS):
            r = ROWS * t
            first = jnp.where(low_lanes, part[r : r + 8], part[r + 8 : r + 16])
            prs[t] = jnp.concatenate([first, part[r + 16 : r + 24]], axis=0).astype(bf16)
        prr[me_t] = prs[me_t]
        to_plane(PR_RS, lambda p: prs.at[p], prr.at[me_t])

    def square_part():
        loads[1].wait()
        aint_v[...] = (2.0 * jnp.transpose(ain_v[0:RANK, :].astype(f32), (1, 0))).astype(bf16)
        loads[2].wait()
        wj_copy.wait()
        squares = jnp.zeros((8, COLS), f32)
        for i in range(NWB):
            rows = slice(WBLK * i, WBLK * (i + 1))
            a = wj_v[rows, :].astype(f32) + dot(aint_v[rows, :], aout_v[0:RANK, my_part], 1, 0)
            squares = squares + jnp.sum((a * a).reshape(WBLK // 8, 8, COLS), axis=0)
        sqr[me_t] = jnp.sum(squares, axis=0, keepdims=True)

    def send_squares():
        to_plane(SQ_RS, lambda p: sqr.at[me_t], sqr.at[me_t])

    def sum_squares():
        got(SQ_RS, sqr.at[fifteen])
        sqf[:, my_part] = sum_of(sqr, PEERS)
        to_group(SQ_AG, lambda p: sqf.at[:, my_part], sqf.at[:, my_part])

    def adjust(i):
        w_copy(i).wait()
        rows = pl.ds(pl.multiple_of(i * WBLK, WBLK), WBLK)
        lhs = aint_v[rows, :]
        for c in range(8):
            cols = slice(512 * c, 512 * (c + 1))
            a = w_v[rows, cols].astype(f32) + dot(lhs, aout_v[0:RANK, cols], 1, 0)
            w_v[rows, cols] = a.astype(bf16)

    def send_columns():
        for h in range(2):
            for d in range(LINE):
                to = slot(h, 0, d)
                low = to < PEERS // 2
                at = pl.ds(pl.multiple_of(lax.rem(to, PEERS // 2) * 128, 128), 128)
                rows = []
                for m in range(LINE):
                    c = cotb[h, y * LINE + m if h == 0 else m * LINE + x, :, at].astype(f32)
                    rows.append(jnp.where(low, c[0:ROWS], c[ROWS : 2 * ROWS]))
                jsend[h, d] = jnp.concatenate(rows, axis=0).astype(bf16)
        for h in range(2):
            me = y if h == 0 else x
            jrecv[h, me] = jsend[h, 0]
            for d in range(1, LINE):
                pltpu.make_async_remote_copy(
                    src_ref=jsend.at[h, d], dst_ref=jrecv.at[h, me], send_sem=ph_send.at[J], recv_sem=ph_recv.at[J],
                    device_id={"tensor": slot(h, 0, d)}, device_id_type=MESH,
                ).start()

    def first_along():
        for h in range(2):
            arrive(h, -1, 0, None, 0)
            go(h, -1, 0, 0, slot(h, 1, 0), 2)
            arrive(h, 1, 0, None, 1)
            go(h, 1, 0, 1, slot(h, -1, 0), 3)

    def last_along():
        for h in range(2):
            arrive(h, 2, 0, 0, 2)
            arrive(h, 2, 0, 1, 3)

    def sum_projected():
        got(PR_RS, prr.at[fifteen])
        total = prr[0].astype(f32)
        for t in range(1, PEERS):
            total = total + prr[t].astype(f32)
        pra[me_t] = total
        to_plane(PR_AG, lambda p: pra.at[me_t], pra.at[me_t])

    def produce(i):
        cols = pl.ds(pl.multiple_of(i * 256, 256), 256)
        prod[:, cols] = dot(hid_v[...], w_v[:, cols], 1, 0)

    def out_grad():
        got(J, jrecv.at[:, pl.ds(0, LINE - 1)])
        got(PR_AG, pra.at[fifteen])
        lanes = lax.broadcasted_iota(jnp.int32, (2 * ROWS, 128), 1) < RANK
        o = []
        for h in range(2):
            for i in range(0, PEERS, 2):

                def three(n):
                    t = n if h == 0 else n % LINE * LINE + n // LINE
                    tile = pra[t, 0:8]
                    turned = pltpu.roll(tile, RANK, 1)
                    return [jnp.where(low_lanes, tile, turned), jnp.where(low_lanes, turned, tile), pra[t, 8:16]]

                rows = jnp.concatenate(three(i) + three(i + 1), axis=0)
                high = rows.astype(bf16).astype(f32)
                lv[ROWS * i : ROWS * (i + 2), :] = jnp.where(lanes, high, rows - high).astype(bf16)
            both = dot(lv[...], jrecv[h].reshape(TOK, 128), 0, 0)
            o.append(both[0:RANK] + both[RANK:])
        for p in range(GROUP):
            opart[p] = o[p % 2][8 * (p // 2) : 8 * (p // 2) + 8]
        orecv[me_d] = opart[me_d]
        to_group(O_RS, lambda p: opart.at[p], orecv.at[me_d])

    def sum_out_grad():
        got(O_RS, orecv.at[fifteen])
        mine = pl.ds(pl.multiple_of(core * HALF + me_t * 128, 128), 128)
        oz[z] = 2.0 * sum_of(orecv, GROUP) * scale_v[:, mine]
        along_z(O_Z, oz.at[z])

    def spread_out_grad():
        got(O_Z, oz.at[pl.ds(0, DEPTH - 1)])
        ob[core, me_t] = oz[...].reshape(RANK, 128).astype(bf16)
        to_plane(O_PL, lambda p: ob.at[core, me_t], ob.at[core, me_t])

    other = swap(O_CORE, ob.at[core])

    def swap_out_grad():
        got(O_PL, ob.at[0, fifteen])
        other.start()

    def column_scale():
        loads[7].wait()
        got(SQ_AG, sqf.at[:, fifteen_cols])
        norm_v[...] = jnp.sqrt(sqf[...] + epsilon)
        scale_v[...] = mag_v[...] / norm_v[...]

    def send_rank():
        loads[6].wait()
        rank = jnp.zeros((32, 128), f32)
        for c in range(8):
            cols = slice(512 * c, 512 * (c + 1))
            s = cot_v[:, cols].astype(f32) * scale_v[:, cols]
            s = jnp.concatenate([s, jnp.zeros((8, 512), f32)], axis=0).astype(bf16)
            rank = rank + dot(s, aout_v[:, cols], 1, 1)
        rcs[...] = jnp.concatenate([jnp.where(low_lanes, rank[0:8], rank[8:16]), rank[16:24]], axis=0).astype(bf16)
        rca[me_t] = rcs[...]
        to_plane(RC_AG, lambda p: rcs, rca.at[me_t])

    def in_grad():
        got(RC_AG, rca.at[fifteen])
        for t in range(0, PEERS, 2):
            c0 = rca[t].astype(f32)
            c1 = rca[t + 1].astype(f32)
            rows = jnp.concatenate(
                [c0[0:8], pltpu.roll(c0[0:8], RANK, 1), c0[8:16], c1[0:8], pltpu.roll(c1[0:8], RANK, 1), c1[8:16]], axis=0
            )
            lv[ROWS * t : ROWS * (t + 2), :] = rows.astype(bf16)
        for g in range(4):
            w = 256 if g < 3 else 128
            o = dot(lv[...], hid_v[:, 256 * g : 256 * g + w], 0, 0).astype(bf16)
            for b in range(4):
                ipart[4 * b + g, :, 0:w] = o[16 * b : 16 * b + 16]
                if w < 256:
                    ipart[4 * b + g, :, w:256] = jnp.zeros((16, 256 - w), bf16)
        irecv[me_d] = ipart[me_d]
        to_group(IN_RS, lambda p: ipart.at[p], irecv.at[me_d])

    def sum_in_grad():
        got(IN_RS, irecv.at[fifteen])
        total = irecv[0].astype(f32)
        for t in range(1, GROUP):
            total = total + irecv[t].astype(f32)
        iag[core, z] = (2.0 * total).astype(bf16)
        along_z(IN_AG, iag.at[core, z])

    other_in = swap(IN_CORE, iag.at[core])

    def swap_in_grad():
        got(IN_AG, iag.at[0, pl.ds(0, DEPTH - 1)])
        other_in.start()

    CH = 256

    def rows_of(s):
        return pl.ds(pl.multiple_of(s * ROWS, ROWS), ROWS)

    def prepare(k):
        for h in range(2):
            for pair in range(2):
                if h == 0:
                    s0 = lax.rem(y + k + 3, LINE) * LINE + 2 * pair
                    s1 = s0 + 1
                else:
                    s0 = 2 * pair * LINE + lax.rem(x + k + 3, LINE)
                    s1 = s0 + LINE

                @pl.loop(0, QUART // CH)
                def _(c):
                    here = pl.ds(pl.multiple_of(c * CH, CH), CH)
                    c0 = cotb[h, s0, :, here].astype(f32)
                    c1 = cotb[h, s1, :, here].astype(f32)
                    for q in range(2):
                        a = c0[ROWS * q : ROWS * (q + 1)]
                        b = c1[ROWS * q : ROWS * (q + 1)]
                        at = pl.multiple_of(HALF * h + QUART * q + c * CH, CH)
                        cols = pl.ds(at, CH)
                        both = jnp.concatenate([a, b], axis=0) * scale_v[:, cols]
                        dst = pl.ds(pl.multiple_of(k * 96 + 48 * pair, 48), 48)
                        scaled[h, dst, pl.ds(pl.multiple_of(QUART * q + c * CH, CH), CH)] = both.astype(bf16)
                        m = a * prod[rows_of(s0), cols] + b * prod[rows_of(s1), cols]
                        magacc[:, cols] += jnp.sum(m.reshape(ROWS // 8, 8, CH), axis=0)

    def multiply(h, first=0, last=F):
        for f in range(first, last, 256):
            w = min(256, F - f)
            r = dot(scaled[h], w_v[f : f + w, HALF * h : HALF * (h + 1)], 1, 1)
            for k in range(LINE):
                block = r[96 * k : 96 * (k + 1)]
                if h == 0:
                    at = pl.multiple_of(lax.rem(y + k + 3, LINE) * 96, 96)
                    hg[pl.ds(at, 96), f : f + w] = block
                else:
                    for yy in range(LINE):
                        s = yy * LINE + lax.rem(x + k + 3, LINE)
                        hg[rows_of(s), f : f + w] += block[ROWS * yy : ROWS * (yy + 1)]

    def send_mag():
        magp[...] = jnp.sum(magacc[...], axis=0, keepdims=True)
        magr[me_t] = magp[:, my_cols(me_t)]
        to_plane(M_RS, lambda p: magp.at[:, my_cols(p)], magr.at[me_t])

    def sum_mag_plane():
        got(M_RS, magr.at[fifteen])
        magd[me_d] = sum_of(magr, PEERS)
        to_group(M_DP, lambda p: magd.at[me_d], magd.at[me_d])

    def sum_mag_group():
        got(M_DP, magd.at[fifteen])
        gmag_v[:, my_cols(me_t)] = sum_of(magd, GROUP) / norm_v[:, my_cols(me_t)]
        to_plane(M_AG, lambda p: gmag_v.at[:, my_cols(me_t)], gmag_v.at[:, my_cols(me_t)])

    outs = [
        pltpu.make_async_copy(out_a, ggate_h, out_sem.at[0]),
        pltpu.make_async_copy(out_b, gup_h, out_sem.at[1]),
        pltpu.make_async_copy(gin_v, gin_h, out_sem.at[2]),
        pltpu.make_async_copy(gout_v, gout_h, out_sem.at[3]),
        pltpu.make_async_copy(gmag_v, gmag_h, out_sem.at[4]),
    ]

    def large_grads():
        @pl.loop(0, TOK // 16)
        def _(i):
            rows = pl.ds(pl.multiple_of(i * 16, 16), 16)
            g = hg[rows, :]
            out_b[rows, :] = (g * u_v[rows, :]).astype(bf16)
            out_a[rows, :] = (g * v_v[rows, :]).astype(bf16)

        outs[0].start()
        outs[1].start()

    def finish_in_grad():
        other_in.wait_recv()
        for b in range(4):
            for g in range(4):
                w, p = 256 if g < 3 else 128, 4 * b + g
                gin_v[16 * b : 16 * b + 16, 256 * g : 256 * g + w] = iag[p % 2, p // 2, :, 0:w].astype(f32)
        outs[2].start()

    def finish_out_grad():
        other.wait_recv()
        for t in range(PEERS):
            for c in range(2):
                at = HALF * c + 128 * t
                gout_v[:, at : at + 128] = ob[c, t].astype(f32)
        outs[3].start()

    def finish_mag():
        got(M_AG, gmag_v.at[:, fifteen_cols])
        outs[4].start()

    pl.semaphore_wait(barrier, PEERS + GROUP - 2)
    for h in range(2):
        go(h, 0, 0, None, slot(h, 1, 0), 0)
        go(h, 0, 0, None, slot(h, -1, 0), 1)
    square_part()
    send_squares()
    gate_and_up()
    project()
    for h in range(2):
        send_across(h, 0)
    pl.loop(0, NWB)(adjust)
    first_along()
    for h in range(2):
        send_across(h, 1)
    pl.loop(0, 5)(produce)
    sum_squares()
    sum_projected()
    for h in range(2):
        send_across(h, 2)
    pl.loop(5, 10)(produce)
    last_along()
    send_columns()
    for h in range(2):
        send_across(h, 3)
    pl.loop(10, 16)(produce)
    column_scale()
    send_rank()
    for h in range(2):
        forward_across(h, 0)
    for h in range(2):
        forward_across(h, 1)
        forward_across(h, 2)
    magacc[...] = jnp.zeros_like(magacc)
    prepare(1)
    out_grad()
    for h in range(2):
        forward_across(h, 3)
    prepare(0)
    prepare(2)
    in_grad()
    for h in range(2):
        for j in range(4):
            last_across(h, j)
    prepare(3)
    send_mag()
    sum_out_grad()
    multiply(0)
    multiply(1, 0, 256)
    sum_mag_plane()
    sum_in_grad()
    spread_out_grad()
    multiply(1, 256, F)
    large_grads()
    sum_mag_group()
    swap_in_grad()
    swap_out_grad()
    finish_in_grad()
    finish_out_grad()
    finish_mag()

    for c in sent:
        c.wait_send()
    other.wait_send()
    left_here(J, jsend.at[:, pl.ds(0, LINE - 1)])
    left_here(SQ_RS, sqr.at[fifteen])
    left_here(SQ_AG, sqf.at[:, fifteen_cols])
    left_here(PR_RS, prs.at[fifteen])
    left_here(PR_AG, pra.at[fifteen])
    left_here(RC_AG, rca.at[fifteen])
    left_here(IN_RS, ipart.at[fifteen])
    left_here(IN_AG, iag.at[0, pl.ds(0, DEPTH - 1)])
    other_in.wait_send()
    left_here(O_RS, opart.at[fifteen])
    left_here(O_PL, ob.at[0, fifteen])
    left_here(O_Z, oz.at[pl.ds(0, DEPTH - 1)])
    left_here(M_RS, magp.at[:, fifteen_cols])
    left_here(M_DP, magd.at[fifteen])
    left_here(M_AG, gmag_v.at[:, fifteen_cols])
    for c in outs:
        c.wait()


PARTS = (4, 4, 1, 8, 1)


def hand_over(*refs):
    src, dst, held, sem_in, sem_out = refs[0:5], refs[5:10], refs[10:15], refs[15], refs[16]
    into, out = [], []
    for i in range(5):
        rows = src[i].shape[0] // PARTS[i]
        for k in range(PARTS[i]):
            part, n = pl.ds(k * rows, rows), len(into)
            into.append(pltpu.make_async_copy(src[i].at[part], held[i].at[part], sem_in.at[n]))
            out.append(pltpu.make_async_copy(held[i].at[part], dst[i].at[part], sem_out.at[n]))
    for c in into:
        c.start()
    for c, d in zip(into, out, strict=True):
        c.wait()
        d.start()
    for d in out:
        d.wait()


def on_device(gate_act, up_act, cotangent, frozen_weight, adapter_in, adapter_out, magnitude):
    V = pltpu.VMEM
    scratch = [
        V((F, D), bf16), V((TOK, F), bf16), V((TOK, F), bf16), V((TOK, F), bf16),
        V((TOK, F), f32), V((TOK, F), f32), V((ROWS, D), bf16),
        V((2 * RANK, F), bf16), V((2 * RANK, D), bf16), V((1, D), f32), V((F, RANK), bf16),
        V((2, PEERS, 48, QUART), bf16), V((2, TOK, HALF), bf16), V((TOK, D), f32), V((TOK, F), f32),
        V((8, D), f32), V((1, D), f32), V((1, D), f32),
        V((2, LINE, 96, 128), bf16), V((2, LINE, 96, 128), bf16),
        V((F, COLS), bf16), V((PEERS, 1, COLS), f32), V((1, D), f32),
        V((PEERS, 16, 128), bf16), V((PEERS, 16, 128), bf16), V((PEERS, 16, 128), f32),
        V((16, 128), bf16), V((PEERS, 16, 128), bf16), V((TOK, 128), bf16),
        V((GROUP, 16, 256), bf16), V((GROUP, 16, 256), bf16), V((2, DEPTH, 16, 256), bf16),
        V((RANK, F), f32), V((GROUP, 8, 128), f32), V((GROUP, 8, 128), f32), V((DEPTH, 8, 128), f32),
        V((2, PEERS, RANK, 128), bf16), V((RANK, D), f32),
        V((1, D), f32), V((PEERS, 1, COLS), f32), V((GROUP, 1, COLS), f32), V((1, D), f32),
        V((TOK, F), bf16), V((TOK, F), bf16),
        pltpu.SemaphoreType.DMA((9,)), pltpu.SemaphoreType.DMA((NWB,)), pltpu.SemaphoreType.DMA((5,)),
        pltpu.SemaphoreType.DMA((N_PHASES,)), pltpu.SemaphoreType.DMA((N_PHASES,)),
        pltpu.SemaphoreType.DMA((40,)), pltpu.SemaphoreType.DMA((40,)),
    ]
    hbm = pl.BlockSpec(memory_space=pl.ANY)
    outs = pl.pallas_call(
        kernel,
        out_shape=(
            jax.ShapeDtypeStruct((TOK, F), bf16),
            jax.ShapeDtypeStruct((TOK, F), bf16),
            jax.ShapeDtypeStruct((RANK, F), f32),
            jax.ShapeDtypeStruct((RANK, D), f32),
            jax.ShapeDtypeStruct((1, D), f32),
        ),
        in_specs=[hbm] * 7,
        out_specs=[hbm] * 5,
        scratch_shapes=scratch,
        compiler_params=pltpu.CompilerParams(
            collective_id=0, has_side_effects=True, vmem_limit_bytes=60 * 1024 * 1024
        ),
        cost_estimate=pl.CostEstimate(flops=7_000_000_000, bytes_accessed=14_000_000, transcendentals=400_000),
    )(gate_act, up_act, cotangent, frozen_weight, adapter_in, adapter_out, magnitude.reshape(1, D))
    outs = pl.pallas_call(
        hand_over,
        out_shape=[jax.ShapeDtypeStruct(o.shape, o.dtype) for o in outs],
        in_specs=[hbm] * 5,
        out_specs=[hbm] * 5,
        scratch_shapes=[V(o.shape, o.dtype) for o in outs]
        + [pltpu.SemaphoreType.DMA((sum(PARTS),)), pltpu.SemaphoreType.DMA((sum(PARTS),))],
        compiler_params=pltpu.CompilerParams(vmem_limit_bytes=60 * 1024 * 1024),
    )(*outs)
    return outs[0], outs[1], outs[2], outs[3], outs[4].reshape(D)


def solution(mesh):
    in_specs = (
        P("dp", "tensor"),
        P("dp", "tensor"),
        P(("dp", "tensor"), None),
        P("tensor", None),
        P(None, "tensor"),
        P(),
        P(),
    )
    out_specs = (P("dp", "tensor"), P("dp", "tensor"), P(None, "tensor"), P(), P())
    return jax.shard_map(
        on_device, mesh=mesh, in_specs=in_specs, out_specs=out_specs, check_vma=False
    )
```

```python
import jax
import jax.numpy as jnp
from jax import lax
from jax.experimental import pallas as pl
from jax.experimental.pallas import tpu as pltpu
from jax.sharding import PartitionSpec as P

epsilon = 1e-06
MESH = pl.DeviceIdType.MESH
f32 = jnp.float32
bf16 = jnp.bfloat16

LINE = 4
PEERS = LINE * LINE
GROUP = 16
DEPTH = GROUP // 2
ROWS = 24
TOK = ROWS * PEERS
F = 896
D = 4096
RANK = 64
HALF = D // 2
QUART = D // 4
COLS = D // PEERS
WBLK = 128
NWB = F // WBLK

(O_LINE, SQ_RS, SQ_AG, PR_RS, PR_AG, RC_AG, IN_RS, IN_AG, O_RS, O_PL, O_Z, O_CORE, M_RS, M_DP, M_AG, IN_CORE) = range(16)
N_PHASES = 16


def dot(a, b, da, db):
    return lax.dot_general(a, b, (((da,), (db,)), ((), ())), preferred_element_type=f32)


def kernel(
    gate_h, up_h, cot_h, w_h, ain_h, aout_h, mag_h,
    ggate_h, gup_h, gin_h, gout_h, gmag_h,
    w_v, gate_v, up_v, hid_v, u_v, v_v, cot_v, ain_v, aout_v, mag_v, aint_v,
    cotb, scaled, prod, hg, magacc, scale_v, norm_v,
    oline_s, oline_r, wj_v, sqr, sqf, prs, prr, pra, rcs, rca, lv,
    ipart, irecv, iag, gin_v, opart, orecv, oz, ob, gout_v,
    magp, magr, magd, gmag_v, out_a, out_b,
    loc_sem, w_sem, out_sem, ph_send, ph_recv, g_send, g_recv,
):
    me_t = lax.axis_index("tensor")
    me_d = lax.axis_index("dp")
    x = lax.rem(me_t, LINE)
    y = lax.div(me_t, LINE)
    z = lax.div(me_d, 2)
    core = lax.rem(me_d, 2)

    barrier = pltpu.get_barrier_semaphore()

    @pl.loop(1, PEERS)
    def _(d):
        pl.semaphore_signal(barrier, inc=1, device_id={"tensor": lax.rem(me_t + d, PEERS)}, device_id_type=MESH)

    @pl.loop(1, GROUP)
    def _(d):
        pl.semaphore_signal(barrier, inc=1, device_id={"dp": lax.rem(me_d + d, GROUP)}, device_id_type=MESH)

    loads = [
        pltpu.make_async_copy(cot_h, cot_v, loc_sem.at[0]),
        pltpu.make_async_copy(ain_h, ain_v.at[pl.ds(0, RANK)], loc_sem.at[1]),
        pltpu.make_async_copy(aout_h, aout_v.at[pl.ds(0, RANK)], loc_sem.at[2]),
        pltpu.make_async_copy(gate_h, gate_v, loc_sem.at[3]),
        pltpu.make_async_copy(up_h, up_v, loc_sem.at[4]),
        pltpu.make_async_copy(ain_h, ain_v.at[pl.ds(RANK, RANK)], loc_sem.at[5]),
        pltpu.make_async_copy(aout_h, aout_v.at[pl.ds(RANK, RANK)], loc_sem.at[6]),
        pltpu.make_async_copy(mag_h, mag_v, loc_sem.at[7]),
    ]

    def w_copy(i):
        rows = pl.ds(pl.multiple_of(i * WBLK, WBLK), WBLK)
        return pltpu.make_async_copy(w_h.at[rows], w_v.at[rows], w_sem.at[i])

    my_part = pl.ds(pl.multiple_of(me_d * COLS, COLS), COLS)
    wj_copy = pltpu.make_async_copy(w_h.at[:, my_part], wj_v, loc_sem.at[8])
    for c in loads[0:3]:
        c.start()
    wj_copy.start()
    for c in loads[3:6]:
        c.start()
    for i in range(NWB):
        w_copy(i).start()
    for c in loads[6:]:
        c.start()

    loads[0].wait()
    for h in range(2):
        left = cot_v[:, HALF * h : HALF * h + QUART].astype(f32)
        right = cot_v[:, HALF * h + QUART : HALF * (h + 1)].astype(f32)
        cotb[h, me_t] = jnp.concatenate([left, right], axis=0).astype(bf16)

    def slot(h, along, across):
        if h == 0:
            return lax.rem(y + across + LINE, LINE) * LINE + lax.rem(x + along + LINE, LINE)
        return lax.rem(y + along + LINE, LINE) * LINE + lax.rem(x + across + LINE, LINE)

    def move(h, along, across, part, to, sem):
        if part is None:
            ref = cotb.at[h, slot(h, along, across)]
        else:
            ref = cotb.at[h, slot(h, along, across), :, pl.ds(part * (QUART // 2), QUART // 2)]
        return pltpu.make_async_remote_copy(
            src_ref=ref, dst_ref=ref, send_sem=g_send.at[20 * h + sem], recv_sem=g_recv.at[20 * h + sem],
            device_id={"tensor": to}, device_id_type=MESH,
        )

    sent = []

    def go(h, along, across, part, to, sem):
        c = move(h, along, across, part, to, sem)
        c.start()
        sent.append(c)

    def arrive(h, along, across, part, sem):
        move(h, along, across, part, slot(h, 0, 1), sem).wait_recv()

    offsets = (0, -1, 1, 2)

    def send_across(h, j):
        go(h, offsets[j], 0, None, slot(h, 0, 1), 4 + 4 * j)
        go(h, offsets[j], 0, None, slot(h, 0, -1), 5 + 4 * j)

    def forward_across(h, j):
        arrive(h, offsets[j], -1, None, 4 + 4 * j)
        go(h, offsets[j], -1, 0, slot(h, 0, 1), 6 + 4 * j)
        arrive(h, offsets[j], 1, None, 5 + 4 * j)
        go(h, offsets[j], 1, 1, slot(h, 0, -1), 7 + 4 * j)

    def last_across(h, j):
        arrive(h, offsets[j], 2, 0, 6 + 4 * j)
        arrive(h, offsets[j], 2, 1, 7 + 4 * j)

    def exchange(phase, axis, src, dst, me, n):
        def one(p):
            return pltpu.make_async_remote_copy(
                src_ref=src(p), dst_ref=dst, send_sem=ph_send.at[phase], recv_sem=ph_recv.at[phase],
                device_id={axis: p}, device_id_type=MESH,
            )

        @pl.loop(1, n)
        def _(d):
            one(lax.rem(me + d, n)).start()

    def got(phase, ref):
        pltpu.make_async_copy(ref, ref, ph_recv.at[phase]).wait()

    def left_here(phase, ref):
        pltpu.make_async_copy(ref, ref, ph_send.at[phase]).wait()

    def to_plane(phase, src, dst):
        exchange(phase, "tensor", src, dst, me_t, PEERS)

    def to_group(phase, src, dst):
        exchange(phase, "dp", src, dst, me_d, GROUP)

    def along_z(phase, ref):
        @pl.loop(1, DEPTH)
        def _(d):
            pltpu.make_async_remote_copy(
                src_ref=ref, dst_ref=ref, send_sem=ph_send.at[phase], recv_sem=ph_recv.at[phase],
                device_id={"dp": lax.rem(z + d, DEPTH) * 2 + core}, device_id_type=MESH,
            ).start()

    def swap(phase, ref):
        return pltpu.make_async_remote_copy(
            src_ref=ref, dst_ref=ref, send_sem=ph_send.at[phase], recv_sem=ph_recv.at[phase],
            device_id={"dp": z * 2 + 1 - core}, device_id_type=MESH,
        )

    def my_cols(p):
        return pl.ds(pl.multiple_of(p * COLS, COLS), COLS)

    fifteen = pl.ds(0, 15)
    fifteen_cols = pl.ds(0, 15 * COLS)

    def sum_of(ref, n):
        total = ref[0]
        for t in range(1, n):
            total = total + ref[t]
        return total

    low_lanes = lax.broadcasted_iota(jnp.int32, (8, 128), 1) < RANK

    def gate_and_up():
        loads[3].wait()
        loads[4].wait()

        @pl.loop(0, TOK // 16)
        def _(i):
            rows = pl.ds(pl.multiple_of(i * 16, 16), 16)
            g = gate_v[rows, :].astype(f32)
            u = up_v[rows, :].astype(f32)
            s = 1.0 / (1.0 + jnp.exp(-g))
            gs = g * s
            hid_v[rows, :] = (gs * u).astype(bf16)
            u_v[rows, :] = gs
            v_v[rows, :] = u * s * (1.0 + g * (1.0 - s))

    def project():
        loads[5].wait()
        part = dot(hid_v[...], ain_v[...], 1, 1)
        for t in range(PEERS):
            r = ROWS * t
            first = jnp.where(low_lanes, part[r : r + 8], part[r + 8 : r + 16])
            prs[t] = jnp.concatenate([first, part[r + 16 : r + 24]], axis=0).astype(bf16)
        prr[me_t] = prs[me_t]
        to_plane(PR_RS, lambda p: prs.at[p], prr.at[me_t])

    def square_part():
        loads[1].wait()
        aint_v[...] = (2.0 * jnp.transpose(ain_v[0:RANK, :].astype(f32), (1, 0))).astype(bf16)
        loads[2].wait()
        wj_copy.wait()
        squares = jnp.zeros((8, COLS), f32)
        for i in range(NWB):
            rows = slice(WBLK * i, WBLK * (i + 1))
            a = wj_v[rows, :].astype(f32) + dot(aint_v[rows, :], aout_v[0:RANK, my_part], 1, 0)
            squares = squares + jnp.sum((a * a).reshape(WBLK // 8, 8, COLS), axis=0)
        sqr[me_t] = jnp.sum(squares, axis=0, keepdims=True)

    def send_squares():
        to_plane(SQ_RS, lambda p: sqr.at[me_t], sqr.at[me_t])

    def sum_squares():
        got(SQ_RS, sqr.at[fifteen])
        sqf[:, my_part] = sum_of(sqr, PEERS)
        to_group(SQ_AG, lambda p: sqf.at[:, my_part], sqf.at[:, my_part])

    def adjust(i):
        w_copy(i).wait()
        rows = pl.ds(pl.multiple_of(i * WBLK, WBLK), WBLK)
        lhs = aint_v[rows, :]
        for c in range(8):
            cols = slice(512 * c, 512 * (c + 1))
            a = w_v[rows, cols].astype(f32) + dot(lhs, aout_v[0:RANK, cols], 1, 0)
            w_v[rows, cols] = a.astype(bf16)

    def first_along():
        for h in range(2):
            arrive(h, -1, 0, None, 0)
            go(h, -1, 0, 0, slot(h, 1, 0), 2)
            arrive(h, 1, 0, None, 1)
            go(h, 1, 0, 1, slot(h, -1, 0), 3)

    def last_along():
        for h in range(2):
            arrive(h, 2, 0, 0, 2)
            arrive(h, 2, 0, 1, 3)

    def sum_projected():
        got(PR_RS, prr.at[fifteen])
        total = prr[0].astype(f32)
        for t in range(1, PEERS):
            total = total + prr[t].astype(f32)
        pra[0, x] = total
        pra[1, y] = total
        for d in range(1, LINE):
            for h, own in ((0, x), (1, y)):
                pltpu.make_async_remote_copy(
                    src_ref=pra.at[h, own], dst_ref=pra.at[h, own],
                    send_sem=ph_send.at[PR_AG], recv_sem=ph_recv.at[PR_AG],
                    device_id={"tensor": slot(h, d, 0)}, device_id_type=MESH,
                ).start()

    def produce(i):
        cols = pl.ds(pl.multiple_of(i * 256, 256), 256)
        prod[:, cols] = dot(hid_v[...], w_v[:, cols], 1, 0)

    def out_grad():
        got(PR_AG, pra.at[:, pl.ds(0, LINE - 1)])
        lanes = lax.broadcasted_iota(jnp.int32, (LINE * ROWS, 128), 1) < RANK
        for h in range(2):
            quarter = x if h == 0 else y
            at = pl.ds(pl.multiple_of(lax.rem(quarter, 2) * 512, 512), 512)
            left, right = [], []
            for m in range(LINE):
                c = cotb[h, y * LINE + m if h == 0 else m * LINE + x, :, at].astype(f32)
                right.append(jnp.where(quarter < 2, c[0:ROWS], c[ROWS : 2 * ROWS]))
                tile = pra[h, m, 0:8]
                turned = pltpu.roll(tile, RANK, 1)
                left += [jnp.where(low_lanes, tile, turned), jnp.where(low_lanes, turned, tile), pra[h, m, 8:16]]
            left = jnp.concatenate(left, axis=0)
            high = left.astype(bf16).astype(f32)
            left = jnp.where(lanes, high, left - high).astype(bf16)
            both = dot(left, jnp.concatenate(right, axis=0).astype(bf16), 0, 0)
            o = both[0:RANK] + both[RANK:]
            for zz in range(DEPTH):
                rows = o[8 * zz : 8 * zz + 8]
                opart[2 * zz + h] = jnp.concatenate([rows[:, 0:256], rows[:, 256:512]], axis=0).astype(bf16)
        orecv[me_d] = opart[me_d]
        to_group(O_RS, lambda p: opart.at[p], orecv.at[me_d])

    in_line = (1 - core) * y + core * x
    off_line = (1 - core) * x + core * y

    def sum_out_grad():
        got(O_RS, orecv.at[fifteen])
        total = orecv[0].astype(f32)
        for t in range(1, GROUP):
            total = total + orecv[t].astype(f32)
        for j in range(LINE):
            oline_s[j] = total[8 * (j // 2) : 8 * (j // 2) + 8, 128 * (j % 2) : 128 * (j % 2) + 128]
        oline_r[in_line] = oline_s[in_line]
        for d in range(1, LINE):
            to = lax.rem(in_line + d, LINE)
            pltpu.make_async_remote_copy(
                src_ref=oline_s.at[to], dst_ref=oline_r.at[in_line],
                send_sem=ph_send.at[O_LINE], recv_sem=ph_recv.at[O_LINE],
                device_id={"tensor": (1 - core) * (to * LINE + x) + core * (y * LINE + to)}, device_id_type=MESH,
            ).start()

    def sum_out_line():
        got(O_LINE, oline_r.at[pl.ds(0, LINE - 1)])
        mine = pl.ds(pl.multiple_of(core * HALF + off_line * 512 + in_line * 128, 128), 128)
        oz[z] = 2.0 * sum_of(oline_r, LINE) * scale_v[:, mine]
        along_z(O_Z, oz.at[z])

    def spread_out_grad():
        got(O_Z, oz.at[pl.ds(0, DEPTH - 1)])
        ob[core, me_t] = oz[...].reshape(RANK, 128).astype(bf16)
        to_plane(O_PL, lambda p: ob.at[core, me_t], ob.at[core, me_t])

    other = swap(O_CORE, ob.at[core])

    def swap_out_grad():
        got(O_PL, ob.at[0, fifteen])
        other.start()

    def column_scale():
        loads[7].wait()
        got(SQ_AG, sqf.at[:, fifteen_cols])
        norm_v[...] = jnp.sqrt(sqf[...] + epsilon)
        scale_v[...] = mag_v[...] / norm_v[...]

    def send_rank():
        loads[6].wait()
        rank = jnp.zeros((32, 128), f32)
        for c in range(8):
            cols = slice(512 * c, 512 * (c + 1))
            s = cot_v[:, cols].astype(f32) * scale_v[:, cols]
            s = jnp.concatenate([s, jnp.zeros((8, 512), f32)], axis=0).astype(bf16)
            rank = rank + dot(s, aout_v[:, cols], 1, 1)
        rcs[...] = jnp.concatenate([jnp.where(low_lanes, rank[0:8], rank[8:16]), rank[16:24]], axis=0).astype(bf16)
        rca[me_t] = rcs[...]
        to_plane(RC_AG, lambda p: rcs, rca.at[me_t])

    def in_grad():
        got(RC_AG, rca.at[fifteen])
        for t in range(0, PEERS, 2):
            c0 = rca[t].astype(f32)
            c1 = rca[t + 1].astype(f32)
            rows = jnp.concatenate(
                [c0[0:8], pltpu.roll(c0[0:8], RANK, 1), c0[8:16], c1[0:8], pltpu.roll(c1[0:8], RANK, 1), c1[8:16]], axis=0
            )
            lv[ROWS * t : ROWS * (t + 2), :] = rows.astype(bf16)
        for g in range(4):
            w = 256 if g < 3 else 128
            o = dot(lv[...], hid_v[:, 256 * g : 256 * g + w], 0, 0).astype(bf16)
            for b in range(4):
                ipart[4 * b + g, :, 0:w] = o[16 * b : 16 * b + 16]
                if w < 256:
                    ipart[4 * b + g, :, w:256] = jnp.zeros((16, 256 - w), bf16)
        irecv[me_d] = ipart[me_d]
        to_group(IN_RS, lambda p: ipart.at[p], irecv.at[me_d])

    def sum_in_grad():
        got(IN_RS, irecv.at[fifteen])
        total = irecv[0].astype(f32)
        for t in range(1, GROUP):
            total = total + irecv[t].astype(f32)
        iag[core, z] = (2.0 * total).astype(bf16)
        along_z(IN_AG, iag.at[core, z])

    other_in = swap(IN_CORE, iag.at[core])

    def swap_in_grad():
        got(IN_AG, iag.at[0, pl.ds(0, DEPTH - 1)])
        other_in.start()

    CH = 256

    def rows_of(s):
        return pl.ds(pl.multiple_of(s * ROWS, ROWS), ROWS)

    def prepare(k):
        for h in range(2):
            for pair in range(2):
                if h == 0:
                    s0 = lax.rem(y + k + 3, LINE) * LINE + 2 * pair
                    s1 = s0 + 1
                else:
                    s0 = 2 * pair * LINE + lax.rem(x + k + 3, LINE)
                    s1 = s0 + LINE

                @pl.loop(0, QUART // CH)
                def _(c):
                    here = pl.ds(pl.multiple_of(c * CH, CH), CH)
                    c0 = cotb[h, s0, :, here].astype(f32)
                    c1 = cotb[h, s1, :, here].astype(f32)
                    for q in range(2):
                        a = c0[ROWS * q : ROWS * (q + 1)]
                        b = c1[ROWS * q : ROWS * (q + 1)]
                        at = pl.multiple_of(HALF * h + QUART * q + c * CH, CH)
                        cols = pl.ds(at, CH)
                        both = jnp.concatenate([a, b], axis=0) * scale_v[:, cols]
                        dst = pl.ds(pl.multiple_of(k * 96 + 48 * pair, 48), 48)
                        scaled[h, dst, pl.ds(pl.multiple_of(QUART * q + c * CH, CH), CH)] = both.astype(bf16)
                        m = a * prod[rows_of(s0), cols] + b * prod[rows_of(s1), cols]
                        magacc[:, cols] += jnp.sum(m.reshape(ROWS // 8, 8, CH), axis=0)

    def multiply(h, first, last):
        def block(f, w):
            units = pl.ds(pl.multiple_of(f, 128), w)
            r = dot(scaled[h], w_v[units, HALF * h : HALF * (h + 1)], 1, 1)
            for k in range(LINE):
                rows = r[96 * k : 96 * (k + 1)]
                if h == 0:
                    at = pl.multiple_of(lax.rem(y + k + 3, LINE) * 96, 96)
                    hg[pl.ds(at, 96), units] = rows
                else:
                    for yy in range(LINE):
                        s = yy * LINE + lax.rem(x + k + 3, LINE)
                        hg[rows_of(s), units] += rows[ROWS * yy : ROWS * (yy + 1)]

        if first < 3:

            @pl.loop(first, min(last, 3))
            def _(i):
                block(i * 256, 256)

        if last == 4:
            block(768, 128)

    def send_mag():
        magp[...] = jnp.sum(magacc[...], axis=0, keepdims=True)
        magr[me_t] = magp[:, my_cols(me_t)]
        to_plane(M_RS, lambda p: magp.at[:, my_cols(p)], magr.at[me_t])

    def sum_mag_plane():
        got(M_RS, magr.at[fifteen])
        magd[me_d] = sum_of(magr, PEERS)
        to_group(M_DP, lambda p: magd.at[me_d], magd.at[me_d])

    def sum_mag_group():
        got(M_DP, magd.at[fifteen])
        gmag_v[:, my_cols(me_t)] = sum_of(magd, GROUP) / norm_v[:, my_cols(me_t)]
        to_plane(M_AG, lambda p: gmag_v.at[:, my_cols(me_t)], gmag_v.at[:, my_cols(me_t)])

    outs = [
        pltpu.make_async_copy(out_a, ggate_h, out_sem.at[0]),
        pltpu.make_async_copy(out_b, gup_h, out_sem.at[1]),
        pltpu.make_async_copy(gin_v, gin_h, out_sem.at[2]),
        pltpu.make_async_copy(gout_v, gout_h, out_sem.at[3]),
        pltpu.make_async_copy(gmag_v, gmag_h, out_sem.at[4]),
    ]

    def large_grads():
        @pl.loop(0, TOK // 16)
        def _(i):
            rows = pl.ds(pl.multiple_of(i * 16, 16), 16)
            g = hg[rows, :]
            out_b[rows, :] = (g * u_v[rows, :]).astype(bf16)
            out_a[rows, :] = (g * v_v[rows, :]).astype(bf16)

        outs[0].start()
        outs[1].start()

    def finish_in_grad():
        other_in.wait_recv()
        for b in range(4):
            for g in range(4):
                w, p = 256 if g < 3 else 128, 4 * b + g
                gin_v[16 * b : 16 * b + 16, 256 * g : 256 * g + w] = iag[p % 2, p // 2, :, 0:w].astype(f32)
        outs[2].start()

    def finish_out_grad():
        other.wait_recv()
        for t in range(PEERS):
            for c in range(2):
                xx, yy = t % LINE, t // LINE
                at = HALF + 512 * yy + 128 * xx if c else 512 * xx + 128 * yy
                gout_v[:, at : at + 128] = ob[c, t].astype(f32)
        outs[3].start()

    def finish_mag():
        got(M_AG, gmag_v.at[:, fifteen_cols])
        outs[4].start()

    pl.semaphore_wait(barrier, PEERS + GROUP - 2)
    for h in range(2):
        go(h, 0, 0, None, slot(h, 1, 0), 0)
        go(h, 0, 0, None, slot(h, -1, 0), 1)
    square_part()
    send_squares()
    gate_and_up()
    project()
    for h in range(2):
        send_across(h, 0)
    pl.loop(0, NWB)(adjust)
    first_along()
    for h in range(2):
        send_across(h, 1)
    pl.loop(0, 5)(produce)
    sum_squares()
    sum_projected()
    for h in range(2):
        send_across(h, 2)
    pl.loop(5, 10)(produce)
    last_along()
    for h in range(2):
        send_across(h, 3)
    pl.loop(10, 13)(produce)
    out_grad()
    pl.loop(13, 16)(produce)
    column_scale()
    send_rank()
    for h in range(2):
        forward_across(h, 0)
    for h in range(2):
        forward_across(h, 1)
        forward_across(h, 2)
    magacc[...] = jnp.zeros_like(magacc)
    prepare(1)
    for h in range(2):
        forward_across(h, 3)
    prepare(0)
    prepare(2)
    sum_out_grad()
    in_grad()
    for h in range(2):
        for j in range(4):
            last_across(h, j)
    prepare(3)
    send_mag()
    multiply(0, 0, 3)
    sum_out_line()
    multiply(0, 3, 4)
    multiply(1, 0, 1)
    sum_mag_plane()
    sum_in_grad()
    spread_out_grad()
    multiply(1, 1, 4)
    large_grads()
    sum_mag_group()
    swap_in_grad()
    swap_out_grad()
    finish_in_grad()
    finish_out_grad()
    finish_mag()

    for c in sent:
        c.wait_send()
    other.wait_send()
    left_here(O_LINE, oline_s.at[pl.ds(0, LINE - 1)])
    left_here(SQ_RS, sqr.at[fifteen])
    left_here(SQ_AG, sqf.at[:, fifteen_cols])
    left_here(PR_RS, prs.at[fifteen])
    left_here(PR_AG, pra.at[:, pl.ds(0, LINE - 1)])
    left_here(RC_AG, rca.at[fifteen])
    left_here(IN_RS, ipart.at[fifteen])
    left_here(IN_AG, iag.at[0, pl.ds(0, DEPTH - 1)])
    other_in.wait_send()
    left_here(O_RS, opart.at[fifteen])
    left_here(O_PL, ob.at[0, fifteen])
    left_here(O_Z, oz.at[pl.ds(0, DEPTH - 1)])
    left_here(M_RS, magp.at[:, fifteen_cols])
    left_here(M_DP, magd.at[fifteen])
    left_here(M_AG, gmag_v.at[:, fifteen_cols])
    for c in outs:
        c.wait()


PARTS = (4, 4, 1, 8, 1)


def hand_over(*refs):
    src, dst, held, sem_in, sem_out = refs[0:5], refs[5:10], refs[10:15], refs[15], refs[16]
    into, out = [], []
    for i in range(5):
        rows = src[i].shape[0] // PARTS[i]
        for k in range(PARTS[i]):
            part, n = pl.ds(k * rows, rows), len(into)
            into.append(pltpu.make_async_copy(src[i].at[part], held[i].at[part], sem_in.at[n]))
            out.append(pltpu.make_async_copy(held[i].at[part], dst[i].at[part], sem_out.at[n]))
    for c in into:
        c.start()
    for c, d in zip(into, out, strict=True):
        c.wait()
        d.start()
    for d in out:
        d.wait()


def on_device(gate_act, up_act, cotangent, frozen_weight, adapter_in, adapter_out, magnitude):
    V = pltpu.VMEM
    scratch = [
        V((F, D), bf16), V((TOK, F), bf16), V((TOK, F), bf16), V((TOK, F), bf16),
        V((TOK, F), f32), V((TOK, F), f32), V((ROWS, D), bf16),
        V((2 * RANK, F), bf16), V((2 * RANK, D), bf16), V((1, D), f32), V((F, RANK), bf16),
        V((2, PEERS, 48, QUART), bf16), V((2, TOK, HALF), bf16), V((TOK, D), f32), V((TOK, F), f32),
        V((8, D), f32), V((1, D), f32), V((1, D), f32),
        V((LINE, 8, 128), f32), V((LINE, 8, 128), f32),
        V((F, COLS), bf16), V((PEERS, 1, COLS), f32), V((1, D), f32),
        V((PEERS, 16, 128), bf16), V((PEERS, 16, 128), bf16), V((2, LINE, 16, 128), f32),
        V((16, 128), bf16), V((PEERS, 16, 128), bf16), V((TOK, 128), bf16),
        V((GROUP, 16, 256), bf16), V((GROUP, 16, 256), bf16), V((2, DEPTH, 16, 256), bf16),
        V((RANK, F), f32), V((GROUP, 16, 256), bf16), V((GROUP, 16, 256), bf16), V((DEPTH, 8, 128), f32),
        V((2, PEERS, RANK, 128), bf16), V((RANK, D), f32),
        V((1, D), f32), V((PEERS, 1, COLS), f32), V((GROUP, 1, COLS), f32), V((1, D), f32),
        V((TOK, F), bf16), V((TOK, F), bf16),
        pltpu.SemaphoreType.DMA((9,)), pltpu.SemaphoreType.DMA((NWB,)), pltpu.SemaphoreType.DMA((5,)),
        pltpu.SemaphoreType.DMA((N_PHASES,)), pltpu.SemaphoreType.DMA((N_PHASES,)),
        pltpu.SemaphoreType.DMA((40,)), pltpu.SemaphoreType.DMA((40,)),
    ]
    hbm = pl.BlockSpec(memory_space=pl.ANY)
    outs = pl.pallas_call(
        kernel,
        out_shape=(
            jax.ShapeDtypeStruct((TOK, F), bf16),
            jax.ShapeDtypeStruct((TOK, F), bf16),
            jax.ShapeDtypeStruct((RANK, F), f32),
            jax.ShapeDtypeStruct((RANK, D), f32),
            jax.ShapeDtypeStruct((1, D), f32),
        ),
        in_specs=[hbm] * 7,
        out_specs=[hbm] * 5,
        scratch_shapes=scratch,
        compiler_params=pltpu.CompilerParams(
            collective_id=0, has_side_effects=True, vmem_limit_bytes=60 * 1024 * 1024
        ),
        cost_estimate=pl.CostEstimate(flops=7_000_000_000, bytes_accessed=14_000_000, transcendentals=400_000),
    )(gate_act, up_act, cotangent, frozen_weight, adapter_in, adapter_out, magnitude.reshape(1, D))
    outs = pl.pallas_call(
        hand_over,
        out_shape=[jax.ShapeDtypeStruct(o.shape, o.dtype) for o in outs],
        in_specs=[hbm] * 5,
        out_specs=[hbm] * 5,
        scratch_shapes=[V(o.shape, o.dtype) for o in outs]
        + [pltpu.SemaphoreType.DMA((sum(PARTS),)), pltpu.SemaphoreType.DMA((sum(PARTS),))],
        compiler_params=pltpu.CompilerParams(vmem_limit_bytes=60 * 1024 * 1024),
    )(*outs)
    return outs[0], outs[1], outs[2], outs[3], outs[4].reshape(D)


def solution(mesh):
    in_specs = (
        P("dp", "tensor"),
        P("dp", "tensor"),
        P(("dp", "tensor"), None),
        P("tensor", None),
        P(None, "tensor"),
        P(),
        P(),
    )
    out_specs = (P("dp", "tensor"), P("dp", "tensor"), P(None, "tensor"), P(), P())
    return jax.shard_map(
        on_device, mesh=mesh, in_specs=in_specs, out_specs=out_specs, check_vma=False
    )
```

```python
import jax
import jax.numpy as jnp
from jax import lax
from jax.experimental import pallas as pl
from jax.experimental.pallas import tpu as pltpu
from jax.sharding import PartitionSpec as P

epsilon = 1e-06
MESH = pl.DeviceIdType.MESH
f32 = jnp.float32
bf16 = jnp.bfloat16

LINE = 4
PEERS = LINE * LINE
GROUP = 16
DEPTH = GROUP // 2
ROWS = 24
TOK = ROWS * PEERS
F = 896
D = 4096
RANK = 64
HALF = D // 2
QUART = D // 4
COLS = D // PEERS
WBLK = 128
NWB = F // WBLK

(O_LINE, SQ_RS, SQ_AG, PR_RS, PR_AG, RC_AG, IN_RS, IN_AG, O_RS, O_PL, O_Z, O_CORE, M_RS, M_DP, M_AG, IN_CORE) = range(16)
N_PHASES = 16


def dot(a, b, da, db):
    return lax.dot_general(a, b, (((da,), (db,)), ((), ())), preferred_element_type=f32)


def kernel(
    gate_h, up_h, cot_h, w_h, ain_h, aout_h, mag_h,
    ggate_h, gup_h, gin_h, gout_h, gmag_h,
    w_v, gate_v, up_v, hid_v, u_v, v_v, cot_v, ain_v, aout_v, mag_v, aint_v,
    cotb, scaled, prod, hg, magacc, scale_v, norm_v,
    oline_s, oline_r, wj_v, sqr, sqf, prs, prr, pra, rcs, rca, lv,
    ipart, irecv, iag, gin_v, opart, orecv, oz, ob, gout_v,
    magp, magr, magd, gmag_v, out_a, out_b,
    loc_sem, w_sem, out_sem, ph_send, ph_recv, g_send, g_recv,
):
    me_t = lax.axis_index("tensor")
    me_d = lax.axis_index("dp")
    x = lax.rem(me_t, LINE)
    y = lax.div(me_t, LINE)
    z = lax.div(me_d, 2)
    core = lax.rem(me_d, 2)

    barrier = pltpu.get_barrier_semaphore()

    @pl.loop(1, PEERS)
    def _(d):
        pl.semaphore_signal(barrier, inc=1, device_id={"tensor": lax.rem(me_t + d, PEERS)}, device_id_type=MESH)

    @pl.loop(1, GROUP)
    def _(d):
        pl.semaphore_signal(barrier, inc=1, device_id={"dp": lax.rem(me_d + d, GROUP)}, device_id_type=MESH)

    loads = [
        pltpu.make_async_copy(cot_h, cot_v, loc_sem.at[0]),
        pltpu.make_async_copy(ain_h, ain_v.at[pl.ds(0, RANK)], loc_sem.at[1]),
        pltpu.make_async_copy(aout_h, aout_v.at[pl.ds(0, RANK)], loc_sem.at[2]),
        pltpu.make_async_copy(gate_h, gate_v, loc_sem.at[3]),
        pltpu.make_async_copy(up_h, up_v, loc_sem.at[4]),
        pltpu.make_async_copy(ain_h, ain_v.at[pl.ds(RANK, RANK)], loc_sem.at[5]),
        pltpu.make_async_copy(aout_h, aout_v.at[pl.ds(RANK, RANK)], loc_sem.at[6]),
        pltpu.make_async_copy(mag_h, mag_v, loc_sem.at[7]),
    ]

    def w_copy(i):
        rows = pl.ds(pl.multiple_of(i * WBLK, WBLK), WBLK)
        return pltpu.make_async_copy(w_h.at[rows], w_v.at[rows], w_sem.at[i])

    my_part = pl.ds(pl.multiple_of(me_d * COLS, COLS), COLS)
    wj_copy = pltpu.make_async_copy(w_h.at[:, my_part], wj_v, loc_sem.at[8])
    for c in loads[0:3]:
        c.start()
    wj_copy.start()
    for c in loads[3:6]:
        c.start()
    for i in range(NWB):
        w_copy(i).start()
    for c in loads[6:]:
        c.start()

    loads[0].wait()
    for h in range(2):
        left = cot_v[:, HALF * h : HALF * h + QUART].astype(f32)
        right = cot_v[:, HALF * h + QUART : HALF * (h + 1)].astype(f32)
        cotb[h, me_t] = jnp.concatenate([left, right], axis=0).astype(bf16)

    def slot(h, along, across):
        if h == 0:
            return lax.rem(y + across + LINE, LINE) * LINE + lax.rem(x + along + LINE, LINE)
        return lax.rem(y + along + LINE, LINE) * LINE + lax.rem(x + across + LINE, LINE)

    def move(h, along, across, part, to, sem):
        if part is None:
            ref = cotb.at[h, slot(h, along, across)]
        else:
            ref = cotb.at[h, slot(h, along, across), :, pl.ds(part * (QUART // 2), QUART // 2)]
        return pltpu.make_async_remote_copy(
            src_ref=ref, dst_ref=ref, send_sem=g_send.at[20 * h + sem], recv_sem=g_recv.at[20 * h + sem],
            device_id={"tensor": to}, device_id_type=MESH,
        )

    sent = []

    def go(h, along, across, part, to, sem):
        c = move(h, along, across, part, to, sem)
        c.start()
        sent.append(c)

    def arrive(h, along, across, part, sem):
        move(h, along, across, part, slot(h, 0, 1), sem).wait_recv()

    offsets = (0, -1, 1, 2)

    def send_across(h, j):
        go(h, offsets[j], 0, None, slot(h, 0, 1), 4 + 4 * j)
        go(h, offsets[j], 0, None, slot(h, 0, -1), 5 + 4 * j)

    def forward_across(h, j):
        arrive(h, offsets[j], -1, None, 4 + 4 * j)
        go(h, offsets[j], -1, 0, slot(h, 0, 1), 6 + 4 * j)
        arrive(h, offsets[j], 1, None, 5 + 4 * j)
        go(h, offsets[j], 1, 1, slot(h, 0, -1), 7 + 4 * j)

    def last_across(h, j):
        arrive(h, offsets[j], 2, 0, 6 + 4 * j)
        arrive(h, offsets[j], 2, 1, 7 + 4 * j)

    def exchange(phase, axis, src, dst, me, n):
        def one(p):
            return pltpu.make_async_remote_copy(
                src_ref=src(p), dst_ref=dst, send_sem=ph_send.at[phase], recv_sem=ph_recv.at[phase],
                device_id={axis: p}, device_id_type=MESH,
            )

        @pl.loop(1, n)
        def _(d):
            one(lax.rem(me + d, n)).start()

    def got(phase, ref):
        pltpu.make_async_copy(ref, ref, ph_recv.at[phase]).wait()

    def left_here(phase, ref):
        pltpu.make_async_copy(ref, ref, ph_send.at[phase]).wait()

    def to_plane(phase, src, dst):
        exchange(phase, "tensor", src, dst, me_t, PEERS)

    def to_group(phase, src, dst):
        exchange(phase, "dp", src, dst, me_d, GROUP)

    def along_z(phase, ref):
        @pl.loop(1, DEPTH)
        def _(d):
            pltpu.make_async_remote_copy(
                src_ref=ref, dst_ref=ref, send_sem=ph_send.at[phase], recv_sem=ph_recv.at[phase],
                device_id={"dp": lax.rem(z + d, DEPTH) * 2 + core}, device_id_type=MESH,
            ).start()

    def swap(phase, ref):
        return pltpu.make_async_remote_copy(
            src_ref=ref, dst_ref=ref, send_sem=ph_send.at[phase], recv_sem=ph_recv.at[phase],
            device_id={"dp": z * 2 + 1 - core}, device_id_type=MESH,
        )

    def my_cols(p):
        return pl.ds(pl.multiple_of(p * COLS, COLS), COLS)

    fifteen = pl.ds(0, 15)
    fifteen_cols = pl.ds(0, 15 * COLS)

    def sum_of(ref, n):
        total = ref[0]
        for t in range(1, n):
            total = total + ref[t]
        return total

    low_lanes = lax.broadcasted_iota(jnp.int32, (8, 128), 1) < RANK

    def gate_and_up():
        loads[3].wait()
        loads[4].wait()

        @pl.loop(0, TOK // 16)
        def _(i):
            rows = pl.ds(pl.multiple_of(i * 16, 16), 16)
            g = gate_v[rows, :].astype(f32)
            u = up_v[rows, :].astype(f32)
            s = 1.0 / (1.0 + jnp.exp(-g))
            gs = g * s
            hid_v[rows, :] = (gs * u).astype(bf16)
            u_v[rows, :] = gs
            v_v[rows, :] = u * s * (1.0 + g * (1.0 - s))

    def project():
        loads[5].wait()
        part = dot(hid_v[...], ain_v[...], 1, 1)
        for t in range(PEERS):
            r = ROWS * t
            first = jnp.where(low_lanes, part[r : r + 8], part[r + 8 : r + 16])
            prs[t] = jnp.concatenate([first, part[r + 16 : r + 24]], axis=0).astype(bf16)
        prr[me_t] = prs[me_t]
        to_plane(PR_RS, lambda p: prs.at[p], prr.at[me_t])

    def square_part():
        loads[1].wait()
        aint_v[...] = (2.0 * jnp.transpose(ain_v[0:RANK, :].astype(f32), (1, 0))).astype(bf16)
        loads[2].wait()
        wj_copy.wait()
        squares = jnp.zeros((8, COLS), f32)
        for i in range(NWB):
            rows = slice(WBLK * i, WBLK * (i + 1))
            a = wj_v[rows, :].astype(f32) + dot(aint_v[rows, :], aout_v[0:RANK, my_part], 1, 0)
            squares = squares + jnp.sum((a * a).reshape(WBLK // 8, 8, COLS), axis=0)
        sqr[me_t] = jnp.sum(squares, axis=0, keepdims=True)

    def send_squares():
        to_plane(SQ_RS, lambda p: sqr.at[me_t], sqr.at[me_t])

    def sum_squares():
        got(SQ_RS, sqr.at[fifteen])
        sqf[:, my_part] = sum_of(sqr, PEERS)
        to_group(SQ_AG, lambda p: sqf.at[:, my_part], sqf.at[:, my_part])

    def adjust(i):
        w_copy(i).wait()
        rows = pl.ds(pl.multiple_of(i * WBLK, WBLK), WBLK)
        lhs = aint_v[rows, :]
        for c in range(8):
            cols = slice(512 * c, 512 * (c + 1))
            a = w_v[rows, cols].astype(f32) + dot(lhs, aout_v[0:RANK, cols], 1, 0)
            w_v[rows, cols] = a.astype(bf16)

    def first_along():
        for h in range(2):
            arrive(h, -1, 0, None, 0)
            go(h, -1, 0, 0, slot(h, 1, 0), 2)
            arrive(h, 1, 0, None, 1)
            go(h, 1, 0, 1, slot(h, -1, 0), 3)

    def last_along():
        for h in range(2):
            arrive(h, 2, 0, 0, 2)
            arrive(h, 2, 0, 1, 3)

    def sum_projected():
        got(PR_RS, prr.at[fifteen])
        total = prr[0].astype(f32)
        for t in range(1, PEERS):
            total = total + prr[t].astype(f32)
        pra[0, x] = total
        pra[1, y] = total
        for d in range(1, LINE):
            for h, own in ((0, x), (1, y)):
                pltpu.make_async_remote_copy(
                    src_ref=pra.at[h, own], dst_ref=pra.at[h, own],
                    send_sem=ph_send.at[PR_AG], recv_sem=ph_recv.at[PR_AG],
                    device_id={"tensor": slot(h, d, 0)}, device_id_type=MESH,
                ).start()

    def produce(i):
        cols = pl.ds(pl.multiple_of(i * 256, 256), 256)
        prod[:, cols] = dot(hid_v[...], w_v[:, cols], 1, 0)

    def out_grad():
        got(PR_AG, pra.at[:, pl.ds(0, LINE - 1)])
        lanes = lax.broadcasted_iota(jnp.int32, (LINE * ROWS, 128), 1) < RANK
        for h in range(2):
            quarter = x if h == 0 else y
            at = pl.ds(pl.multiple_of(lax.rem(quarter, 2) * 512, 512), 512)
            left, right = [], []
            for m in range(LINE):
                c = cotb[h, y * LINE + m if h == 0 else m * LINE + x, :, at].astype(f32)
                right.append(jnp.where(quarter < 2, c[0:ROWS], c[ROWS : 2 * ROWS]))
                tile = pra[h, m, 0:8]
                turned = pltpu.roll(tile, RANK, 1)
                left += [jnp.where(low_lanes, tile, turned), jnp.where(low_lanes, turned, tile), pra[h, m, 8:16]]
            left = jnp.concatenate(left, axis=0)
            high = left.astype(bf16).astype(f32)
            left = jnp.where(lanes, high, left - high).astype(bf16)
            both = dot(left, jnp.concatenate(right, axis=0).astype(bf16), 0, 0)
            o = both[0:RANK] + both[RANK:]
            for zz in range(DEPTH):
                rows = o[8 * zz : 8 * zz + 8]
                opart[2 * zz + h] = jnp.concatenate([rows[:, 0:256], rows[:, 256:512]], axis=0).astype(bf16)
        orecv[me_d] = opart[me_d]
        to_group(O_RS, lambda p: opart.at[p], orecv.at[me_d])

    in_line = (1 - core) * y + core * x
    off_line = (1 - core) * x + core * y

    def sum_out_grad():
        got(O_RS, orecv.at[fifteen])
        total = orecv[0].astype(f32)
        for t in range(1, GROUP):
            total = total + orecv[t].astype(f32)
        for j in range(LINE):
            oline_s[j] = total[8 * (j // 2) : 8 * (j // 2) + 8, 128 * (j % 2) : 128 * (j % 2) + 128]
        oline_r[in_line] = oline_s[in_line]
        for d in range(1, LINE):
            to = lax.rem(in_line + d, LINE)
            pltpu.make_async_remote_copy(
                src_ref=oline_s.at[to], dst_ref=oline_r.at[in_line],
                send_sem=ph_send.at[O_LINE], recv_sem=ph_recv.at[O_LINE],
                device_id={"tensor": (1 - core) * (to * LINE + x) + core * (y * LINE + to)}, device_id_type=MESH,
            ).start()

    def sum_out_line():
        got(O_LINE, oline_r.at[pl.ds(0, LINE - 1)])
        mine = pl.ds(pl.multiple_of(core * HALF + off_line * 512 + in_line * 128, 128), 128)
        oz[z] = 2.0 * sum_of(oline_r, LINE) * scale_v[:, mine]
        along_z(O_Z, oz.at[z])

    def spread_out_grad():
        got(O_Z, oz.at[pl.ds(0, DEPTH - 1)])
        ob[core, me_t] = oz[...].reshape(RANK, 128).astype(bf16)
        to_plane(O_PL, lambda p: ob.at[core, me_t], ob.at[core, me_t])

    other = swap(O_CORE, ob.at[core])

    def swap_out_grad():
        got(O_PL, ob.at[0, fifteen])
        other.start()

    def column_scale():
        loads[7].wait()
        got(SQ_AG, sqf.at[:, fifteen_cols])
        norm_v[...] = jnp.sqrt(sqf[...] + epsilon)
        scale_v[...] = mag_v[...] / norm_v[...]

    def send_rank():
        loads[6].wait()
        rank = jnp.zeros((32, 128), f32)
        for c in range(8):
            cols = slice(512 * c, 512 * (c + 1))
            s = cot_v[:, cols].astype(f32) * scale_v[:, cols]
            s = jnp.concatenate([s, jnp.zeros((8, 512), f32)], axis=0).astype(bf16)
            rank = rank + dot(s, aout_v[:, cols], 1, 1)
        rcs[...] = jnp.concatenate([jnp.where(low_lanes, rank[0:8], rank[8:16]), rank[16:24]], axis=0).astype(bf16)
        rca[me_t] = rcs[...]
        to_plane(RC_AG, lambda p: rcs, rca.at[me_t])

    def in_grad():
        got(RC_AG, rca.at[fifteen])
        for t in range(0, PEERS, 2):
            c0 = rca[t].astype(f32)
            c1 = rca[t + 1].astype(f32)
            rows = jnp.concatenate(
                [c0[0:8], pltpu.roll(c0[0:8], RANK, 1), c0[8:16], c1[0:8], pltpu.roll(c1[0:8], RANK, 1), c1[8:16]], axis=0
            )
            lv[ROWS * t : ROWS * (t + 2), :] = rows.astype(bf16)
        for g in range(4):
            w = 256 if g < 3 else 128
            o = dot(lv[...], hid_v[:, 256 * g : 256 * g + w], 0, 0).astype(bf16)
            for b in range(4):
                ipart[4 * b + g, :, 0:w] = o[16 * b : 16 * b + 16]
                if w < 256:
                    ipart[4 * b + g, :, w:256] = jnp.zeros((16, 256 - w), bf16)
        irecv[me_d] = ipart[me_d]
        to_group(IN_RS, lambda p: ipart.at[p], irecv.at[me_d])

    def sum_in_grad():
        got(IN_RS, irecv.at[fifteen])
        total = irecv[0].astype(f32)
        for t in range(1, GROUP):
            total = total + irecv[t].astype(f32)
        iag[core, z] = (2.0 * total).astype(bf16)
        along_z(IN_AG, iag.at[core, z])

    other_in = swap(IN_CORE, iag.at[core])

    def swap_in_grad():
        got(IN_AG, iag.at[0, pl.ds(0, DEPTH - 1)])
        other_in.start()

    CH = 256

    def rows_of(s):
        return pl.ds(pl.multiple_of(s * ROWS, ROWS), ROWS)

    def prepare(k):
        for h in range(2):
            for pair in range(2):
                if h == 0:
                    s0 = lax.rem(y + k + 3, LINE) * LINE + 2 * pair
                    s1 = s0 + 1
                else:
                    s0 = 2 * pair * LINE + lax.rem(x + k + 3, LINE)
                    s1 = s0 + LINE

                @pl.loop(0, QUART // CH)
                def _(c):
                    here = pl.ds(pl.multiple_of(c * CH, CH), CH)
                    c0 = cotb[h, s0, :, here].astype(f32)
                    c1 = cotb[h, s1, :, here].astype(f32)
                    for q in range(2):
                        a = c0[ROWS * q : ROWS * (q + 1)]
                        b = c1[ROWS * q : ROWS * (q + 1)]
                        at = pl.multiple_of(HALF * h + QUART * q + c * CH, CH)
                        cols = pl.ds(at, CH)
                        both = jnp.concatenate([a, b], axis=0) * scale_v[:, cols]
                        dst = pl.ds(pl.multiple_of(k * 96 + 48 * pair, 48), 48)
                        scaled[h, dst, pl.ds(pl.multiple_of(QUART * q + c * CH, CH), CH)] = both.astype(bf16)
                        m = a * prod[rows_of(s0), cols] + b * prod[rows_of(s1), cols]
                        magacc[:, cols] += jnp.sum(m.reshape(ROWS // 8, 8, CH), axis=0)

    def multiply(h, first, last):
        def block(f, w):
            units = pl.ds(pl.multiple_of(f, 128), w)
            r = dot(scaled[h], w_v[units, HALF * h : HALF * (h + 1)], 1, 1)
            for k in range(LINE):
                rows = r[96 * k : 96 * (k + 1)]
                if h == 0:
                    at = pl.multiple_of(lax.rem(y + k + 3, LINE) * 96, 96)
                    hg[pl.ds(at, 96), units] = rows
                else:
                    for yy in range(LINE):
                        s = yy * LINE + lax.rem(x + k + 3, LINE)
                        hg[rows_of(s), units] += rows[ROWS * yy : ROWS * (yy + 1)]

        if first < 3:

            @pl.loop(first, min(last, 3))
            def _(i):
                block(i * 256, 256)

        if last == 4:
            block(768, 128)

    def send_mag():
        magp[...] = jnp.sum(magacc[...], axis=0, keepdims=True)
        magr[me_t] = magp[:, my_cols(me_t)]
        to_plane(M_RS, lambda p: magp.at[:, my_cols(p)], magr.at[me_t])

    def sum_mag_plane():
        got(M_RS, magr.at[fifteen])
        magd[me_d] = sum_of(magr, PEERS)
        to_group(M_DP, lambda p: magd.at[me_d], magd.at[me_d])

    def sum_mag_group():
        got(M_DP, magd.at[fifteen])
        gmag_v[:, my_cols(me_t)] = sum_of(magd, GROUP) / norm_v[:, my_cols(me_t)]
        to_plane(M_AG, lambda p: gmag_v.at[:, my_cols(me_t)], gmag_v.at[:, my_cols(me_t)])

    outs = [
        pltpu.make_async_copy(out_a, ggate_h, out_sem.at[0]),
        pltpu.make_async_copy(out_b, gup_h, out_sem.at[1]),
        pltpu.make_async_copy(gin_v, gin_h, out_sem.at[2]),
        pltpu.make_async_copy(gout_v, gout_h, out_sem.at[3]),
        pltpu.make_async_copy(gmag_v, gmag_h, out_sem.at[4]),
    ]

    def large_grads():
        @pl.loop(0, TOK // 16)
        def _(i):
            rows = pl.ds(pl.multiple_of(i * 16, 16), 16)
            g = hg[rows, :]
            out_b[rows, :] = (g * u_v[rows, :]).astype(bf16)
            out_a[rows, :] = (g * v_v[rows, :]).astype(bf16)

        outs[0].start()
        outs[1].start()

    def finish_in_grad():
        other_in.wait_recv()
        for b in range(4):
            for g in range(4):
                w, p = 256 if g < 3 else 128, 4 * b + g
                gin_v[16 * b : 16 * b + 16, 256 * g : 256 * g + w] = iag[p % 2, p // 2, :, 0:w].astype(f32)
        outs[2].start()

    def finish_out_grad():
        other.wait_recv()
        for t in range(PEERS):
            for c in range(2):
                xx, yy = t % LINE, t // LINE
                at = HALF + 512 * yy + 128 * xx if c else 512 * xx + 128 * yy
                gout_v[:, at : at + 128] = ob[c, t].astype(f32)
        outs[3].start()

    def finish_mag():
        got(M_AG, gmag_v.at[:, fifteen_cols])
        outs[4].start()

    pl.semaphore_wait(barrier, PEERS + GROUP - 2)
    for h in range(2):
        go(h, 0, 0, None, slot(h, 1, 0), 0)
        go(h, 0, 0, None, slot(h, -1, 0), 1)
    square_part()
    send_squares()
    gate_and_up()
    project()
    for h in range(2):
        send_across(h, 0)
    pl.loop(0, NWB)(adjust)
    first_along()
    for h in range(2):
        send_across(h, 1)
    pl.loop(0, 5)(produce)
    sum_squares()
    sum_projected()
    for h in range(2):
        send_across(h, 2)
    pl.loop(5, 10)(produce)
    last_along()
    for h in range(2):
        send_across(h, 3)
    pl.loop(10, 13)(produce)
    out_grad()
    pl.loop(13, 16)(produce)
    column_scale()
    send_rank()
    for h in range(2):
        forward_across(h, 0)
    for h in range(2):
        forward_across(h, 1)
        forward_across(h, 2)
    magacc[...] = jnp.zeros_like(magacc)
    prepare(1)
    for h in range(2):
        forward_across(h, 3)
    prepare(0)
    prepare(2)
    sum_out_grad()
    in_grad()
    for h in range(2):
        for j in range(4):
            last_across(h, j)
    prepare(3)
    send_mag()
    multiply(0, 0, 3)
    sum_out_line()
    multiply(0, 3, 4)
    multiply(1, 0, 1)
    sum_mag_plane()
    multiply(1, 1, 4)
    sum_in_grad()
    spread_out_grad()
    large_grads()
    sum_mag_group()
    swap_in_grad()
    swap_out_grad()
    finish_in_grad()
    finish_out_grad()
    finish_mag()

    for c in sent:
        c.wait_send()
    other.wait_send()
    left_here(O_LINE, oline_s.at[pl.ds(0, LINE - 1)])
    left_here(SQ_RS, sqr.at[fifteen])
    left_here(SQ_AG, sqf.at[:, fifteen_cols])
    left_here(PR_RS, prs.at[fifteen])
    left_here(PR_AG, pra.at[:, pl.ds(0, LINE - 1)])
    left_here(RC_AG, rca.at[fifteen])
    left_here(IN_RS, ipart.at[fifteen])
    left_here(IN_AG, iag.at[0, pl.ds(0, DEPTH - 1)])
    other_in.wait_send()
    left_here(O_RS, opart.at[fifteen])
    left_here(O_PL, ob.at[0, fifteen])
    left_here(O_Z, oz.at[pl.ds(0, DEPTH - 1)])
    left_here(M_RS, magp.at[:, fifteen_cols])
    left_here(M_DP, magd.at[fifteen])
    left_here(M_AG, gmag_v.at[:, fifteen_cols])
    for c in outs:
        c.wait()


PARTS = (4, 4, 1, 8, 1)


def hand_over(*refs):
    src, dst, held, sem_in, sem_out = refs[0:5], refs[5:10], refs[10:15], refs[15], refs[16]
    into, out = [], []
    for i in range(5):
        rows = src[i].shape[0] // PARTS[i]
        for k in range(PARTS[i]):
            part, n = pl.ds(k * rows, rows), len(into)
            into.append(pltpu.make_async_copy(src[i].at[part], held[i].at[part], sem_in.at[n]))
            out.append(pltpu.make_async_copy(held[i].at[part], dst[i].at[part], sem_out.at[n]))
    for c in into:
        c.start()
    for c, d in zip(into, out, strict=True):
        c.wait()
        d.start()
    for d in out:
        d.wait()


def on_device(gate_act, up_act, cotangent, frozen_weight, adapter_in, adapter_out, magnitude):
    V = pltpu.VMEM
    scratch = [
        V((F, D), bf16), V((TOK, F), bf16), V((TOK, F), bf16), V((TOK, F), bf16),
        V((TOK, F), f32), V((TOK, F), f32), V((ROWS, D), bf16),
        V((2 * RANK, F), bf16), V((2 * RANK, D), bf16), V((1, D), f32), V((F, RANK), bf16),
        V((2, PEERS, 48, QUART), bf16), V((2, TOK, HALF), bf16), V((TOK, D), f32), V((TOK, F), f32),
        V((8, D), f32), V((1, D), f32), V((1, D), f32),
        V((LINE, 8, 128), f32), V((LINE, 8, 128), f32),
        V((F, COLS), bf16), V((PEERS, 1, COLS), f32), V((1, D), f32),
        V((PEERS, 16, 128), bf16), V((PEERS, 16, 128), bf16), V((2, LINE, 16, 128), f32),
        V((16, 128), bf16), V((PEERS, 16, 128), bf16), V((TOK, 128), bf16),
        V((GROUP, 16, 256), bf16), V((GROUP, 16, 256), bf16), V((2, DEPTH, 16, 256), bf16),
        V((RANK, F), f32), V((GROUP, 16, 256), bf16), V((GROUP, 16, 256), bf16), V((DEPTH, 8, 128), f32),
        V((2, PEERS, RANK, 128), bf16), V((RANK, D), f32),
        V((1, D), f32), V((PEERS, 1, COLS), f32), V((GROUP, 1, COLS), f32), V((1, D), f32),
        V((TOK, F), bf16), V((TOK, F), bf16),
        pltpu.SemaphoreType.DMA((9,)), pltpu.SemaphoreType.DMA((NWB,)), pltpu.SemaphoreType.DMA((5,)),
        pltpu.SemaphoreType.DMA((N_PHASES,)), pltpu.SemaphoreType.DMA((N_PHASES,)),
        pltpu.SemaphoreType.DMA((40,)), pltpu.SemaphoreType.DMA((40,)),
    ]
    hbm = pl.BlockSpec(memory_space=pl.ANY)
    outs = pl.pallas_call(
        kernel,
        out_shape=(
            jax.ShapeDtypeStruct((TOK, F), bf16),
            jax.ShapeDtypeStruct((TOK, F), bf16),
            jax.ShapeDtypeStruct((RANK, F), f32),
            jax.ShapeDtypeStruct((RANK, D), f32),
            jax.ShapeDtypeStruct((1, D), f32),
        ),
        in_specs=[hbm] * 7,
        out_specs=[hbm] * 5,
        scratch_shapes=scratch,
        compiler_params=pltpu.CompilerParams(
            collective_id=0, has_side_effects=True, vmem_limit_bytes=60 * 1024 * 1024
        ),
        cost_estimate=pl.CostEstimate(flops=7_000_000_000, bytes_accessed=14_000_000, transcendentals=400_000),
    )(gate_act, up_act, cotangent, frozen_weight, adapter_in, adapter_out, magnitude.reshape(1, D))
    outs = pl.pallas_call(
        hand_over,
        out_shape=[jax.ShapeDtypeStruct(o.shape, o.dtype) for o in outs],
        in_specs=[hbm] * 5,
        out_specs=[hbm] * 5,
        scratch_shapes=[V(o.shape, o.dtype) for o in outs]
        + [pltpu.SemaphoreType.DMA((sum(PARTS),)), pltpu.SemaphoreType.DMA((sum(PARTS),))],
        compiler_params=pltpu.CompilerParams(vmem_limit_bytes=60 * 1024 * 1024),
    )(*outs)
    return outs[0], outs[1], outs[2], outs[3], outs[4].reshape(D)


def solution(mesh):
    in_specs = (
        P("dp", "tensor"),
        P("dp", "tensor"),
        P(("dp", "tensor"), None),
        P("tensor", None),
        P(None, "tensor"),
        P(),
        P(),
    )
    out_specs = (P("dp", "tensor"), P("dp", "tensor"), P(None, "tensor"), P(), P())
    return jax.shard_map(
        on_device, mesh=mesh, in_specs=in_specs, out_specs=out_specs, check_vma=False
    )
```
